128 devices in a mesh: dp: 8 (over x, core), tensor: 16 (over y, z).
Axes of the slice: x: 4, y: 4, z: 4, core: 2. Of those that a mesh axis runs over, the one named last changes fastest.
Arguments:
- text_hidden: bfloat16 [2048, 8192], P('dp', 'tensor'), may hold values from -6 to 6
- norm_gain: bfloat16 [8192], P('tensor'), may hold values from 0.5 to 1.5
- gate_alpha: float32 [8192], P('tensor'), may hold values from 0.3 to 1.5
- latents: bfloat16 [8, 64, 8192], P('dp', None, 'tensor'), may hold values from -6 to 6
- query_weight: bfloat16 [8192, 4096], P(None, 'tensor'), may hold values from -0.0625 to 0.0625
- key_weight: bfloat16 [8192, 4096], P(None, 'tensor'), may hold values from -0.0625 to 0.0625
- value_weight: bfloat16 [8192, 4096], P(None, 'tensor'), may hold values from -0.0625 to 0.0625
- out_weight: bfloat16 [4096, 8192], P('tensor'), may hold values from -0.375 to 0.375
- citations: int32 [16, 4], P('dp'), may hold values from 0 to 7, all different within a row
- image_slot: int32 [8], replicated, may hold values from 0 to 7, each once
- out_grad: bfloat16 [2048, 8192], P('dp', 'tensor'), may hold values from -6 to 6
Outputs:
- layer_out: bfloat16 [2048, 8192], P('dp', 'tensor')
- text_grad: bfloat16 [2048, 8192], P('dp', 'tensor')
- query_weight_grad: bfloat16 [8192, 4096], P('dp', 'tensor')
- key_weight_grad: bfloat16 [8192, 4096], P('dp', 'tensor')
- value_weight_grad: bfloat16 [8192, 4096], P('dp', 'tensor')
- out_weight_grad: bfloat16 [4096, 8192], P('tensor', 'dp')
- gain_grad: float32 [8192], P('tensor')
- gate_grad: float32 [8192], P('tensor')
The draws below stay inside these ranges and needn't reach their ends.
Inputs may be any that keep to these rules, and one draw needn't show every extreme that they name: `citations`: each row lists 4 different image ids; every image id is cited by some span. `image_slot`: a permutation; image id i is held in slot image_slot[i] of latents.
All inputs are finite; a program needn't handle non-finite values.
Results may differ from the reference program's by a relative error of at most 0.02.
Values may be sent and summed in bfloat16 or wider, within the bound.
No kernel may reach another device: no remote copies, remote signals or barrier semaphores. Data moves between devices by JAX's collectives and lax.ppermute only.
A program may use at most 128 MiB of HBM per device.

```python
import jax
import jax.numpy as jnp
from jax import lax

D = 8192
HEADS = 32
HEAD_DIM = 128
LAT = 64
CITES = 4
SPAN = 128
IMG_DEV = 1
TXT_DEV = 256
TEXT = 2048
SPANS = 16
IMAGES = 8
HD = 4096
N_DP = 8
N_TENSOR = 16


def block_scale(stream_key, extent, split, least, top_value):
    factor_of, own = 1.0, jax.random.fold_in(stream_key, 6)
    for axis_at, parts in split:
        draws = jnp.exp(jax.random.uniform(jax.random.fold_in(own, axis_at), (parts,), jnp.float32, least / len(split), top_value / len(split)))
        factor_of = factor_of * jnp.repeat(draws, extent[axis_at] // parts).reshape([-1 if axis == axis_at else 1 for axis in range(len(extent))])
    return factor_of


def different_ones(rng, rows, number_of, top, lift):
    order = jax.random.permutation(jax.random.fold_in(rng, 1), number_of)
    boost = order
    for power in range(3):
        boost = boost * boost // number_of
    boost = boost * lift // number_of
    chance = jax.random.randint(jax.random.fold_in(rng, 2), (rows, number_of), 0, 4096) + boost
    fixed_rows = jax.random.permutation(jax.random.fold_in(rng, 3), rows)[jnp.arange(number_of) % rows]
    chance = jnp.where(jnp.arange(rows)[:, None] == fixed_rows[None, :], 1 << 14, chance)
    priority = chance * number_of + jnp.arange(number_of)
    return lax.top_k(priority.astype(jnp.int32), top)[1].astype(jnp.int32)


def gaussian(rng, dims, spread, reach, shards=(), held_as=jnp.bfloat16):
    factor_of = block_scale(rng, dims, shards, -0.22, 0.18) if shards else 1.0
    array = jax.random.normal(rng, dims, jnp.float32) * spread * factor_of
    return jnp.minimum(jnp.maximum(array, -reach), reach).astype(held_as)


def setup_inputs(seed: int = 0) -> dict:
    seeds = jax.random.split(jax.random.key(seed), 12)
    text_hidden = gaussian(seeds[0], (TEXT, D), 1.0, 6.0, ((0, 8), (1, 16)))
    norm_gain = jnp.clip(1.0 + 0.1 * jax.random.normal(seeds[1], (D,), jnp.float32), 0.5, 1.5).astype(jnp.bfloat16)
    gate_alpha = jnp.clip(0.3 + 1.2 * jax.random.uniform(seeds[2], (D,), jnp.float32) ** block_scale(seeds[2], (D,), ((0, 16),), -0.2, 0.2), 0.3, 1.5)
    latents = gaussian(seeds[3], (IMAGES, LAT, D), 1.0, 6.0, ((0, 8), (2, 16)))
    query_weight = gaussian(seeds[4], (D, HD), D ** -0.5, 0.0625, ((1, 16),))
    key_weight = gaussian(seeds[5], (D, HD), D ** -0.5, 0.0625, ((1, 16),))
    value_weight = gaussian(seeds[6], (D, HD), D ** -0.5, 0.0625, ((1, 16),))
    out_weight = gaussian(seeds[7], (HD, D), (HD // 16) ** -0.5, 0.375, ((0, 16),))
    citations = different_ones(seeds[8], SPANS, IMAGES, CITES, 8192)
    image_slot = jax.random.permutation(seeds[9], IMAGES).astype(jnp.int32)
    out_grad = gaussian(seeds[10], (TEXT, D), 1.0, 6.0, ((0, 8), (1, 16)))
    return {"text_hidden": text_hidden, "norm_gain": norm_gain, "gate_alpha": gate_alpha, "latents": latents, "query_weight": query_weight, "key_weight": key_weight, "value_weight": value_weight, "out_weight": out_weight, "citations": citations, "image_slot": image_slot, "out_grad": out_grad}


EPSILON = 1e-05

def rounded(operand):
    return lax.optimization_barrier(operand.astype(jnp.bfloat16)).astype(jnp.float32)

def reference(text_hidden, norm_gain, gate_alpha, latents, query_weight, key_weight, value_weight, out_weight, citations, image_slot, out_grad):
    hidden = text_hidden.astype(jnp.float32)
    inverse_rms = lax.rsqrt(lax.optimization_barrier(jnp.mean(hidden * hidden, axis=1, keepdims=True)) + EPSILON)
    unit_rows = hidden * inverse_rms
    normed = (unit_rows * norm_gain.astype(jnp.float32)).astype(jnp.bfloat16)
    queries = jnp.dot(normed, query_weight, preferred_element_type=jnp.float32).astype(jnp.bfloat16)
    flat_latents = latents.reshape(IMAGES * LAT, D)
    key_rows = jnp.dot(flat_latents, key_weight, preferred_element_type=jnp.float32).astype(jnp.bfloat16)
    value_rows = jnp.dot(flat_latents, value_weight, preferred_element_type=jnp.float32).astype(jnp.bfloat16)
    cited_slots = jnp.take(image_slot, citations, axis=0).astype(jnp.int32)
    span_keys = jnp.take(key_rows.reshape(IMAGES, LAT, HD), cited_slots, axis=0)
    span_keys = span_keys.reshape(SPANS, CITES * LAT, HEADS, HEAD_DIM).astype(jnp.float32)
    span_values = jnp.take(value_rows.reshape(IMAGES, LAT, HD), cited_slots, axis=0)
    span_values = span_values.reshape(SPANS, CITES * LAT, HEADS, HEAD_DIM).astype(jnp.float32)
    query_blocks = queries.reshape(SPANS, SPAN, HEADS, HEAD_DIM).astype(jnp.float32)
    score_scale = HEAD_DIM ** (-0.5)
    scores = jnp.einsum('cqhd,ckhd->chqk', query_blocks, span_keys) * score_scale
    attn_probs = jax.nn.softmax(scores, axis=-1)
    probs_low = rounded(attn_probs)
    attended = jnp.einsum('chqk,ckhd->cqhd', probs_low, span_values).reshape(TEXT, HD).astype(jnp.bfloat16)
    group_cols = HD // N_TENSOR
    branch = jnp.zeros((TEXT, D), jnp.float32)
    for head_group in range(N_TENSOR):
        first_col = head_group * group_cols
        branch = branch + rounded(jnp.dot(attended[:, first_col:first_col + group_cols], out_weight[first_col:first_col + group_cols], preferred_element_type=jnp.float32))
    tanh_gate = jnp.tanh(gate_alpha)
    layer_out = (tanh_gate * branch).astype(jnp.bfloat16)
    upstream = out_grad.astype(jnp.float32)
    gate_grad = lax.optimization_barrier(jnp.sum(upstream * branch, axis=0)) * (1.0 - tanh_gate * tanh_gate)
    branch_grad = (upstream * tanh_gate).astype(jnp.bfloat16)
    attended_grad = jnp.dot(branch_grad, out_weight.T, preferred_element_type=jnp.float32).astype(jnp.bfloat16)
    out_weight_grad = jnp.zeros((HD, D), jnp.float32)
    query_weight_grad = jnp.zeros((D, HD), jnp.float32)
    grad_blocks = attended_grad.reshape(SPANS, SPAN, HEADS, HEAD_DIM).astype(jnp.float32)
    probs_grad = jnp.einsum('cqhd,ckhd->chqk', grad_blocks, span_values)
    score_grad = attn_probs * (probs_grad - lax.optimization_barrier(jnp.sum(attn_probs * probs_grad, axis=-1, keepdims=True)))
    score_low = rounded(score_grad * score_scale)
    query_grad = jnp.einsum('chqk,ckhd->cqhd', score_low, span_keys).reshape(TEXT, HD).astype(jnp.bfloat16)
    key_span = jnp.einsum('chqk,cqhd->ckhd', score_low, query_blocks).reshape(SPANS * CITES, LAT * HD)
    value_span = jnp.einsum('chqk,cqhd->ckhd', probs_low, grad_blocks).reshape(SPANS * CITES, LAT * HD)
    flat_slots = cited_slots.reshape(SPANS * CITES)
    key_grad_rows = jnp.zeros((IMAGES, LAT * HD), jnp.float32).at[flat_slots].add(key_span)
    key_grad_rows = key_grad_rows.astype(jnp.bfloat16).reshape(IMAGES * LAT, HD)
    value_grad_rows = jnp.zeros((IMAGES, LAT * HD), jnp.float32).at[flat_slots].add(value_span)
    value_grad_rows = value_grad_rows.astype(jnp.bfloat16).reshape(IMAGES * LAT, HD)
    key_weight_grad = jnp.zeros((D, HD), jnp.float32)
    value_weight_grad = jnp.zeros((D, HD), jnp.float32)
    owner_rows = IMG_DEV * LAT
    for owner_index in range(N_DP):
        first_tok = owner_index * TXT_DEV
        out_weight_grad = out_weight_grad + rounded(jnp.dot(attended[first_tok:first_tok + TXT_DEV].T, branch_grad[first_tok:first_tok + TXT_DEV], preferred_element_type=jnp.float32))
        query_weight_grad = query_weight_grad + rounded(jnp.dot(normed[first_tok:first_tok + TXT_DEV].T, query_grad[first_tok:first_tok + TXT_DEV], preferred_element_type=jnp.float32))
        first_row = owner_index * owner_rows
        owned = flat_latents[first_row:first_row + owner_rows].T
        key_weight_grad = key_weight_grad + rounded(jnp.dot(owned, key_grad_rows[first_row:first_row + owner_rows], preferred_element_type=jnp.float32))
        value_weight_grad = value_weight_grad + rounded(jnp.dot(owned, value_grad_rows[first_row:first_row + owner_rows], preferred_element_type=jnp.float32))
    normed_grad = jnp.zeros((TEXT, D), jnp.float32)
    for head_group in range(N_TENSOR):
        first_col = head_group * group_cols
        normed_grad = normed_grad + rounded(jnp.dot(query_grad[:, first_col:first_col + group_cols], query_weight[:, first_col:first_col + group_cols].T, preferred_element_type=jnp.float32))
    gain_grad = lax.optimization_barrier(jnp.sum(normed_grad * unit_rows, axis=0))
    unit_grad = normed_grad * norm_gain.astype(jnp.float32)
    row_mean = lax.optimization_barrier(jnp.mean(unit_grad * unit_rows, axis=1, keepdims=True))
    text_grad = ((unit_grad - unit_rows * row_mean) * inverse_rms).astype(jnp.bfloat16)
    return (layer_out, text_grad, query_weight_grad.astype(jnp.bfloat16), key_weight_grad.astype(jnp.bfloat16), value_weight_grad.astype(jnp.bfloat16), out_weight_grad.astype(jnp.bfloat16), gain_grad, gate_grad)
```

```python
import jax
import jax.numpy as jnp
from jax import lax
from jax.sharding import PartitionSpec as P

D = 8192
HEAD_DIM = 128
SIDE = 4
CORES = 2
EPSILON = 1e-05

BF = jnp.bfloat16
F32 = jnp.float32


def contract_rows(left, right):
    return lax.dot_general(left, right, (((0,), (0,)), ((), ())), preferred_element_type=F32)


def contract_cols(left, right):
    return lax.dot_general(left, right, (((1,), (1,)), ((), ())), preferred_element_type=F32)


def send_z(value, by):
    pairs = [(t, t // SIDE * SIDE + (t + by) % SIDE) for t in range(SIDE * SIDE)]
    return lax.ppermute(value, "tensor", pairs)


def send_y(value, by):
    pairs = [(t, (t + by * SIDE) % (SIDE * SIDE)) for t in range(SIDE * SIDE)]
    return lax.ppermute(value, "tensor", pairs)


def send_x(value, by):
    count = SIDE * CORES
    return lax.ppermute(value, "dp", [(i, (i + by * CORES) % count) for i in range(count)])


def send_core(value):
    return lax.ppermute(value, "dp", [(i, i ^ 1) for i in range(SIDE * CORES)])


def send_latents_home(value):
    moves = []
    for i in range(8):
        for t in range(16):
            moves.append((i * 16 + t, (t // 2) * 16 + i * 2 + t % 2))
    return lax.ppermute(value, ("dp", "tensor"), moves)


def take(value, at, axis):
    return lax.dynamic_index_in_dim(value, at, axis, keepdims=False)


def gather_direct(value, send, at):
    others = [(1, send(value, -1)), (3, send(value, 1)), (2, send(value, 2))]
    out = jnp.zeros((SIDE,) + value.shape, value.dtype)
    out = lax.dynamic_update_index_in_dim(out, value, at, 0)
    for step, block in others:
        out = lax.dynamic_update_index_in_dim(out, block, (at + step) % SIDE, 0)
    return out


def gather_ring(value, send):
    half = value.shape[0] // 2
    below = send(value, 1)
    above = send(value, -1)
    low = send(below[:half], 1)
    high = send(above[half:], -1)
    return [value, above, jnp.concatenate([low, high], 0), below]


def add(*terms):
    total = terms[0].astype(F32)
    for term in terms[1:]:
        total = total + term.astype(F32)
    return total


def scatter_ring(parts, send):
    half = parts[2].shape[0] // 2
    low = send(parts[2][:half], 1)
    high = send(parts[2][half:], -1)
    up = jnp.concatenate([add(parts[1][:half], low).astype(BF), parts[1][half:]], 0)
    down = jnp.concatenate([parts[3][:half], add(parts[3][half:], high).astype(BF)], 0)
    return add(parts[0], send(up, 1), send(down, -1))


def scatter_direct(parts, send):
    arrived = [send(parts[2], 2), send(parts[1], 1), send(parts[3], -1)]
    return add(parts[0], *arrived)


def scatter_dp(blocks, core, x):
    given = take(blocks, 1 - core, 1)
    kept = take(blocks, core, 1)
    both = add(kept, send_core(given)).astype(BF)
    return scatter_direct([take(both, (x + k) % SIDE, 0) for k in range(SIDE)], send_x)


def sum_dp(value):
    both = value + send_core(value)
    return both + send_x(both, 1) + send_x(both, -1) + send_x(both, 2)


def sum_tensor(value):
    row = value + send_z(value, 1) + send_z(value, -1) + send_z(value, 2)
    return row + send_y(row, 1) + send_y(row, -1) + send_y(row, 2)


def shards(
    text_hidden,
    norm_gain,
    gate_alpha,
    latents,
    query_weight,
    key_weight,
    value_weight,
    out_weight,
    citations,
    image_slot,
    out_grad,
):
    place, lane = lax.axis_index("dp"), lax.axis_index("tensor")
    x, core = place // CORES, place % CORES
    y, z = lane // SIDE, lane % SIDE
    rows, width = text_hidden.shape
    head_cols = query_weight.shape[1]
    head_count = head_cols // HEAD_DIM
    latent_count = latents.shape[1]
    own_latents = latents.reshape(latent_count, width)

    tanh_gate = jnp.tanh(gate_alpha)
    upstream = out_grad.astype(F32)
    own_branch_grad = (upstream * tanh_gate).astype(BF)

    slice_latents = send_latents_home(own_latents)
    gain_rows = jnp.broadcast_to(norm_gain[None, :], (16, width))
    small = jnp.concatenate([own_latents, gain_rows], 0)
    small_z = gather_direct(small, send_z, z)
    text_z = gather_direct(text_hidden, send_z, z)
    grad_y = gather_direct(jnp.concatenate([own_branch_grad, slice_latents], 0), send_y, y)

    small_all = gather_direct(small_z, send_y, y).reshape(16, latent_count + 16, width)
    full_latents = small_all[:, :latent_count].transpose(1, 0, 2).reshape(latent_count, D)
    full_gain = small_all[:, latent_count].reshape(D)

    text_z = text_z.transpose(1, 0, 2).reshape(rows, SIDE * width)
    full_text = jnp.zeros((rows, D), BF)
    for step, block in enumerate(gather_ring(text_z, send_y)):
        start = (y + step) % SIDE * (SIDE * width)
        full_text = lax.dynamic_update_slice(full_text, block, (0, start))

    grad_y = grad_y.transpose(1, 0, 2)
    grad_all = jnp.zeros((rows + latent_count, SIDE, SIDE, width), BF)
    for step, block in enumerate(gather_ring(grad_y, send_z)):
        grad_all = lax.dynamic_update_slice(
            grad_all, block[:, :, None, :], (0, 0, (z + step) % SIDE, 0)
        )
    branch_grad = grad_all[:rows].reshape(rows, D)
    slice_latents = grad_all[rows:].reshape(latent_count, 8, 2, width)
    slice_latents = slice_latents.transpose(1, 0, 2, 3).reshape(8 * latent_count, 2 * width)

    own_keys = jnp.dot(full_latents, key_weight, preferred_element_type=F32).astype(BF)
    own_values = jnp.dot(full_latents, value_weight, preferred_element_type=F32).astype(BF)
    own_pair = jnp.concatenate([own_keys, own_values], 1)
    other_pair = send_core(own_pair)
    chip_pair = jnp.where(
        core == 0, jnp.stack([own_pair, other_pair]), jnp.stack([other_pair, own_pair])
    )
    all_pair = gather_direct(chip_pair, send_x, x).reshape(8, latent_count, 2 * head_cols)

    hidden = full_text.astype(F32)
    inverse_rms = lax.rsqrt(jnp.mean(hidden * hidden, axis=1, keepdims=True) + EPSILON)
    normed = (hidden * inverse_rms * full_gain.astype(F32)).astype(BF)
    queries = jnp.dot(normed, query_weight, preferred_element_type=F32).astype(BF)

    span_count, cite_count = citations.shape
    cited_slots = jnp.take(image_slot, citations, axis=0)
    span_pair = jnp.take(all_pair, cited_slots, axis=0)
    span_pair = span_pair.reshape(span_count, cite_count * latent_count, 2, head_count, HEAD_DIM)
    span_keys, span_values = span_pair[:, :, 0], span_pair[:, :, 1]
    query_blocks = queries.reshape(span_count, rows // span_count, head_count, HEAD_DIM)
    score_scale = HEAD_DIM ** (-0.5)
    scores = (
        jnp.einsum("cqhd,ckhd->chqk", query_blocks, span_keys, preferred_element_type=F32)
        * score_scale
    )
    attn_probs = jax.nn.softmax(scores, axis=-1)
    probs_low = attn_probs.astype(BF)
    attended = jnp.einsum("chqk,ckhd->cqhd", probs_low, span_values, preferred_element_type=F32)
    attended = attended.astype(BF).reshape(rows, head_cols)

    branch_parts = []
    for step in range(SIDE):
        weight = lax.dynamic_slice_in_dim(
            out_weight, (y + step) % SIDE * (SIDE * width), SIDE * width, 1
        )
        branch_parts.append(jnp.dot(attended, weight, preferred_element_type=F32).astype(BF))
    branch_row = scatter_ring(branch_parts, send_y).astype(BF).reshape(rows, SIDE, width)
    branch = scatter_direct([take(branch_row, (z + k) % SIDE, 1) for k in range(SIDE)], send_z)
    layer_out = (tanh_gate * branch).astype(BF)
    gate_part = jnp.sum(upstream * branch, axis=0) * (1.0 - tanh_gate * tanh_gate)

    attended_grad = contract_cols(branch_grad, out_weight).astype(BF)
    grad_blocks = attended_grad.reshape(query_blocks.shape)
    probs_grad = jnp.einsum(
        "cqhd,ckhd->chqk", grad_blocks, span_values, preferred_element_type=F32
    )
    score_grad = attn_probs * (
        probs_grad - jnp.sum(attn_probs * probs_grad, axis=-1, keepdims=True)
    )
    score_low = (score_grad * score_scale).astype(BF)
    query_grad = jnp.einsum("chqk,ckhd->cqhd", score_low, span_keys, preferred_element_type=F32)
    query_grad = query_grad.astype(BF).reshape(rows, head_cols)

    weight_rows = query_weight.reshape(SIDE, SIDE, width, head_cols)
    normed_parts = []
    for step in range(SIDE):
        weight = take(weight_rows, (z + step) % SIDE, 1).reshape(SIDE * width, head_cols)
        normed_parts.append(contract_cols(query_grad, weight).astype(BF))
    normed_row = scatter_ring(normed_parts, send_z).astype(BF).reshape(rows, SIDE, width)
    normed_grad = scatter_direct([take(normed_row, (y + k) % SIDE, 1) for k in range(SIDE)], send_y)
    row_dot = sum_tensor(jnp.sum(query_grad.astype(F32) * queries.astype(F32), axis=1))

    out_term = contract_rows(attended, branch_grad).astype(BF)
    out_term = out_term.reshape(head_cols, SIDE, CORES, D // 8).transpose(1, 2, 0, 3)
    out_weight_grad = scatter_dp(out_term, core, x).astype(BF)

    key_span = jnp.einsum("chqk,cqhd->ckhd", score_low, query_blocks, preferred_element_type=F32)
    value_span = jnp.einsum("chqk,cqhd->ckhd", probs_low, grad_blocks, preferred_element_type=F32)
    pair_span = jnp.stack([key_span, value_span], 2).reshape(
        span_count * cite_count, latent_count, 2 * head_cols
    )
    pair_part = jnp.zeros((8, latent_count, 2 * head_cols), F32)
    pair_part = pair_part.at[cited_slots.reshape(-1)].add(pair_span)
    pair_part = pair_part.astype(BF).reshape(CORES, 4 * latent_count, 2 * head_cols)
    given = take(pair_part, 1 - core, 0)
    kept = take(pair_part, core, 0)
    pair_half = add(kept, send_core(given)).astype(BF)
    pair_half = add(
        pair_half, send_x(pair_half, 1), send_x(pair_half, -1), send_x(pair_half, 2)
    ).astype(BF)
    pair_other = send_core(pair_half)
    pair_grad = jnp.where(
        core == 0,
        jnp.concatenate([pair_half, pair_other], 0),
        jnp.concatenate([pair_other, pair_half], 0),
    )
    latent_grad = contract_rows(slice_latents, pair_grad).astype(BF)
    key_weight_grad = latent_grad[:, :head_cols]
    value_weight_grad = latent_grad[:, head_cols:]

    query_term = contract_rows(normed, query_grad).astype(BF)
    query_term = query_term.reshape(SIDE, CORES, D // 8, head_cols)
    query_weight_grad = scatter_dp(query_term, core, x).astype(BF)

    own_unit = text_hidden.astype(F32) * inverse_rms
    unit_grad = normed_grad * norm_gain.astype(F32)
    text_grad = ((unit_grad - own_unit * (row_dot / D)[:, None]) * inverse_rms).astype(BF)
    gain_part = jnp.sum(normed_grad * own_unit, axis=0)
    sums = sum_dp(jnp.stack([gain_part, gate_part]))
    return (
        layer_out,
        text_grad,
        query_weight_grad,
        key_weight_grad,
        value_weight_grad,
        out_weight_grad,
        sums[0],
        sums[1],
    )


def solution(mesh):
    placed = (
        P("dp", "tensor"),
        P("tensor"),
        P("tensor"),
        P("dp", None, "tensor"),
        P(None, "tensor"),
        P(None, "tensor"),
        P(None, "tensor"),
        P("tensor", None),
        P("dp", None),
        P(),
        P("dp", "tensor"),
    )
    return jax.shard_map(
        shards,
        mesh=mesh,
        in_specs=placed,
        out_specs=(
            P("dp", "tensor"),
            P("dp", "tensor"),
            P("dp", "tensor"),
            P("dp", "tensor"),
            P("dp", "tensor"),
            P("tensor", "dp"),
            P("tensor"),
            P("tensor"),
        ),
        check_vma=False,
    )
```

```python
import functools

import jax
import jax.numpy as jnp
from jax import lax
from jax.experimental import pallas as pl
from jax.experimental.pallas import tpu as pltpu
from jax.sharding import PartitionSpec as P

D = 8192
HEAD_DIM = 128
SIDE = 4
CORES = 2
LAT = 64
ROWS = 256
WIDTH = 512
COLS = 256
EXTRA = 16
EPSILON = 1e-05
SCALE = HEAD_DIM ** (-0.5)

BF = jnp.bfloat16
F32 = jnp.float32


def dot(left, right, over):
    return lax.dot_general(left, right, ((over[:1], over[1:]), ((), ())), preferred_element_type=F32)


def send_z(value, by):
    pairs = [(t, t // SIDE * SIDE + (t + by) % SIDE) for t in range(SIDE * SIDE)]
    return lax.ppermute(value, "tensor", pairs)


def send_y(value, by):
    pairs = [(t, (t + by * SIDE) % (SIDE * SIDE)) for t in range(SIDE * SIDE)]
    return lax.ppermute(value, "tensor", pairs)


def send_x(value, by):
    count = SIDE * CORES
    return lax.ppermute(value, "dp", [(i, (i + by * CORES) % count) for i in range(count)])


def send_core(value):
    return lax.ppermute(value, "dp", [(i, i ^ 1) for i in range(SIDE * CORES)])


def send_latents_home(value):
    moves = []
    for i in range(8):
        for t in range(16):
            moves.append((i * 16 + t, (t // 2) * 16 + i * 2 + t % 2))
    return lax.ppermute(value, ("dp", "tensor"), moves)


def hold(*values):
    return lax.optimization_barrier(values)


def gather_direct(value, send):
    above, below, across = send(value, -1), send(value, 1), send(value, 2)
    return [value, above, across, below]


def add(*terms):
    total = terms[0].astype(F32)
    for term in terms[1:]:
        total = total + term.astype(F32)
    return total


def feature_block(pos, ky, kz):
    return lax.rem(pos[2] + ky, SIDE) * SIDE + lax.rem(pos[3] + kz, SIDE)


def call(body, pos, grid, ins, outs, scratch, flops, moved):
    arrays, in_specs = zip(*ins)
    shapes, out_specs = zip(*outs)
    return pl.pallas_call(
        body,
        grid_spec=pltpu.PrefetchScalarGridSpec(
            num_scalar_prefetch=1,
            grid=grid,
            in_specs=list(in_specs),
            out_specs=list(out_specs),
            scratch_shapes=scratch,
        ),
        out_shape=list(shapes),
        compiler_params=pltpu.CompilerParams(
            dimension_semantics=("arbitrary",) * len(grid), vmem_limit_bytes=40 * 2**20
        ),
        cost_estimate=pl.CostEstimate(flops=flops, bytes_accessed=moved, transcendentals=0),
    )(pos, *arrays)


def whole(array):
    zeros = (0,) * array.ndim
    return array, pl.BlockSpec(array.shape, lambda *_: zeros)


def whole_out(shape, dtype):
    zeros = (0,) * len(shape)
    return jax.ShapeDtypeStruct(shape, dtype), pl.BlockSpec(shape, lambda *_: zeros)


def query_body(count, first, last, pos, *refs):
    pieces, gains, weights = refs[:count], refs[count : 2 * count], refs[2 * count : 3 * count]
    rest = refs[3 * count :]
    if not first:
        total_in, squares_in, *rest = rest
    out_a, out_b, total, squares = rest
    step = pl.program_id(0)

    @pl.when(step == 0)
    def _():
        if first:
            total[...] = jnp.zeros_like(total)
            squares[...] = jnp.zeros_like(squares)
        else:
            total[...] = total_in[...]
            squares[...] = squares_in[...]

    for piece, gain, weight in zip(pieces, gains, weights):
        text = piece[0].astype(F32)
        square = text * text
        squares[...] += (square[:, :128] + square[:, 128:256]) + (
            square[:, 256:384] + square[:, 384:]
        )
        scaled = (text * gain[0][:1].astype(F32)).astype(BF)
        total[...] += dot(scaled, weight[...], (1, 0))

    @pl.when(step == pl.num_programs(0) - 1)
    def _():
        if last:
            mean = jnp.sum(squares[...], axis=1, keepdims=True) / D
            inverse = lax.rsqrt(mean + EPSILON)
            out_a[...] = (total[...] * inverse).astype(BF)
            out_b[...] = jnp.broadcast_to(inverse, out_b.shape)
        else:
            out_a[...] = total[...]
            out_b[...] = squares[...]


def query_part(pos, arrays, places, small, weight, carry, last):
    steps = arrays[0].shape[0]
    ins = [(a, pl.BlockSpec((1, ROWS, WIDTH), lambda i, pos: (i, 0, 0))) for a in arrays]
    for ky, kz in places:
        at = ky * SIDE + kz
        ins.append((small, pl.BlockSpec((1, EXTRA, WIDTH), lambda i, pos, at=at: (at + i, 4, 0))))
    for ky, kz in places:
        index = lambda i, pos, ky=ky, kz=kz: (feature_block(pos, ky, kz + i), 0)
        ins.append((weight, pl.BlockSpec((WIDTH, COLS), index)))
    ins += [whole(value) for value in carry]
    outs = [
        whole_out((ROWS, COLS), BF if last else F32),
        whole_out((ROWS, 128), F32),
    ]
    scratch = [pltpu.VMEM((ROWS, COLS), F32), pltpu.VMEM((ROWS, 128), F32)]
    body = functools.partial(query_body, len(arrays), not carry, last)
    work = steps * len(arrays)
    return call(body, pos, (steps,), ins, outs, scratch, work * 2 * ROWS * WIDTH * COLS, work * 2**19)


def grad_body(count, first, last, pos, *refs):
    pieces, weights, rest = refs[:count], refs[count : 2 * count], refs[2 * count :]
    if not first:
        total_in, *rest = rest
    out, total = rest
    step = pl.program_id(0)

    @pl.when(step == 0)
    def _():
        total[...] = jnp.zeros_like(total) if first else total_in[...]

    for piece, weight in zip(pieces, weights):
        total[...] += dot(piece[0], weight[...], (1, 1))

    @pl.when(step == pl.num_programs(0) - 1)
    def _():
        out[...] = total[...].astype(out.dtype)


def grad_part(pos, arrays, places, weight, carry, last):
    steps = arrays[0].shape[0]
    ins = [(a, pl.BlockSpec((1, ROWS, WIDTH), lambda i, pos: (i, 0, 0))) for a in arrays]
    for kz, ky in places:
        index = lambda i, pos, ky=ky, kz=kz: (0, feature_block(pos, ky + i, kz))
        ins.append((weight, pl.BlockSpec((COLS, WIDTH), index)))
    ins += [whole(value) for value in carry]
    outs = [whole_out((ROWS, COLS), BF if last else F32)]
    body = functools.partial(grad_body, len(arrays), not carry, last)
    work = steps * len(arrays)
    scratch = [pltpu.VMEM((ROWS, COLS), F32)]
    return call(body, pos, (steps,), ins, outs, scratch, work * 2 * ROWS * WIDTH * COLS, work * 2**19)


def pair_body(pos, small, *refs):
    keys, values, out, total = refs[:SIDE], refs[SIDE : 2 * SIDE], refs[-2], refs[-1]
    step = pl.program_id(0)

    @pl.when(step == 0)
    def _():
        total[...] = jnp.zeros_like(total)

    for kz in range(SIDE):
        latents = small[kz, :LAT]
        total[:, :COLS] += dot(latents, keys[kz][...], (1, 0))
        total[:, COLS:] += dot(latents, values[kz][...], (1, 0))

    @pl.when(step == SIDE - 1)
    def _():
        out[...] = total[...].astype(BF)


def own_pair(pos, small, key_weight, value_weight):
    rows = small.shape[1]
    ins = [(small, pl.BlockSpec((SIDE, rows, WIDTH), lambda i, pos: (i, 0, 0)))]
    for weight in (key_weight, value_weight):
        for kz in range(SIDE):
            index = lambda i, pos, kz=kz: (feature_block(pos, i, kz), 0)
            ins.append((weight, pl.BlockSpec((WIDTH, COLS), index)))
    outs = [whole_out((LAT, 2 * COLS), BF)]
    scratch = [pltpu.VMEM((LAT, 2 * COLS), F32)]
    return call(pair_body, pos, (SIDE,), ins, outs, scratch, 2 * LAT * D * 512, 10 * 2**20)[0]


def attention_body(slots, queries, grads, pair, attended, query_grad, kept, given, row_dot, part):
    part[...] = jnp.zeros_like(part)
    span = ROWS // 2
    ones = jnp.ones((8, COLS), F32)
    for c in range(2):
        rows = slice(c * span, (c + 1) * span)
        places = [slots[c * 4 + j] for j in range(4)]
        blocks = [pair[at] for at in places]
        product, key_grads, value_grads = [], [], []
        for h in range(2):
            cols = slice(h * HEAD_DIM, (h + 1) * HEAD_DIM)
            value_cols = slice(COLS + h * HEAD_DIM, COLS + (h + 1) * HEAD_DIM)
            keys = jnp.concatenate([block[:, cols] for block in blocks], 0)
            values = jnp.concatenate([block[:, value_cols] for block in blocks], 0)
            query, grad = queries[rows, cols], grads[rows, cols]
            scores = dot(query, keys, (1, 1)) * SCALE
            scores = jnp.exp(scores - jnp.max(scores, axis=1, keepdims=True))
            probs = scores / jnp.sum(scores, axis=1, keepdims=True)
            probs_low = probs.astype(BF)
            attended[rows, cols] = dot(probs_low, values, (1, 0)).astype(BF)
            probs_grad = dot(grad, values, (1, 1))
            inner = jnp.sum(probs * probs_grad, axis=1, keepdims=True)
            score_low = (probs * (probs_grad - inner) * SCALE).astype(BF)
            out = dot(score_low, keys, (1, 0)).astype(BF)
            query_grad[rows, cols] = out
            product.append(out.astype(F32) * query.astype(F32))
            key_grads.append(dot(score_low, query, (0, 0)))
            value_grads.append(dot(probs_low, grad, (0, 0)))
        pair_grad = jnp.concatenate(key_grads + value_grads, 1)
        for j in range(4):
            part[places[j]] += pair_grad[j * LAT : (j + 1) * LAT]
        line = lax.dot_general(
            ones,
            jnp.concatenate(product, 1),
            (((1,), (1,)), ((), ())),
            precision=lax.Precision.HIGHEST,
            preferred_element_type=F32,
        )
        row_dot[:, rows] = jnp.concatenate([line, line], 0).astype(BF)
    row_dot[:, ROWS:] = jnp.zeros((EXTRA, WIDTH - ROWS), BF)
    for kx in range(SIDE):
        kept[kx] = part[kx * CORES].astype(BF)
        given[kx] = part[kx * CORES + 1].astype(BF)


def attention(slots, queries, grads, pair):
    ins = [whole(queries), whole(grads), whole(pair)]
    outs = [
        whole_out((ROWS, COLS), BF),
        whole_out((ROWS, COLS), BF),
        whole_out((SIDE, LAT, 2 * COLS), BF),
        whole_out((SIDE, LAT, 2 * COLS), BF),
        whole_out((EXTRA, WIDTH), BF),
    ]
    scratch = [pltpu.VMEM((SIDE * CORES, LAT, 2 * COLS), F32)]
    return call(attention_body, slots, (1,), ins, outs, scratch, 4 * 10 * 2**23, 3 * 2**20)


def parts_body(count, over, pos, left, *refs):
    weights, rest = refs[:count], refs[count:]
    tail = None
    if len(rest) > count:
        tail, *rest = rest
    for weight, out in zip(weights, rest):
        out[0, :ROWS] = dot(left[...], weight[...], over).astype(BF)
        if tail is not None:
            out[0, ROWS:] = tail[...]


def branch_parts(pos, left, weight, steps, places):
    ins = [whole(left)]
    outs = []
    for ky, kz in places:
        index = lambda i, pos, ky=ky, kz=kz: (0, feature_block(pos, ky, kz + i))
        ins.append((weight, pl.BlockSpec((COLS, WIDTH), index)))
        shape = jax.ShapeDtypeStruct((steps, ROWS, WIDTH), BF)
        outs.append((shape, pl.BlockSpec((1, ROWS, WIDTH), lambda i, pos: (i, 0, 0))))
    body = functools.partial(parts_body, len(places), (1, 0))
    work = steps * len(places)
    return call(body, pos, (steps,), ins, outs, [], work * 2 * ROWS * WIDTH * COLS, work * 2**19)


def normed_parts(pos, left, tail, weight, steps, places):
    ins = [whole(left)]
    outs = []
    for kz, ky in places:
        index = lambda i, pos, ky=ky, kz=kz: (feature_block(pos, ky + i, kz), 0)
        ins.append((weight, pl.BlockSpec((WIDTH, COLS), index)))
        shape = jax.ShapeDtypeStruct((steps, ROWS + EXTRA, WIDTH), BF)
        outs.append((shape, pl.BlockSpec((1, ROWS + EXTRA, WIDTH), lambda i, pos: (i, 0, 0))))
    ins.append(whole(tail))
    body = functools.partial(parts_body, len(places), (1, 1))
    work = steps * len(places)
    return call(body, pos, (steps,), ins, outs, [], work * 2 * ROWS * WIDTH * COLS, work * 2**19)


def target_piece(pos, g, other):
    core = 1 - pos[1] if other else pos[1]
    ky = lax.rem(pos[0] + g // 2 + SIDE - pos[2], SIDE)
    kz = lax.rem(core * 2 + g % 2 + SIDE - pos[3], SIDE)
    return ky, kz


def out_weight_body(pos, attended, piece, out):
    out[0] = dot(attended[...], piece[0], (0, 0)).astype(BF)


def out_weight_terms(pos, attended, grads, other):
    def index(g, pos):
        ky, kz = target_piece(pos, g, other)
        return kz * SIDE + ky, 0, 0

    ins = [whole(attended), (grads, pl.BlockSpec((1, ROWS, WIDTH), index))]
    shape = jax.ShapeDtypeStruct((SIDE, COLS, 2 * WIDTH), BF)
    outs = [(shape, pl.BlockSpec((1, COLS, WIDTH), lambda g, pos: (g // 2, 0, g % 2)))]
    return call(out_weight_body, pos, (8,), ins, outs, [], 8 * 2**26, 8 * 2**19)[0]


def query_weight_body(pos, query_grad, inverse, gain, piece, out):
    scale = jnp.concatenate([inverse[...]] * 4, 1)
    normed = (piece[0].astype(F32) * scale * gain[0][:1].astype(F32)).astype(BF)
    out[0] = dot(normed, query_grad[...], (0, 0)).astype(BF)


def query_weight_terms(pos, query_grad, inverse, small, text, other):
    def place(g, pos):
        ky, kz = target_piece(pos, g, other)
        return ky * SIDE + kz

    ins = [
        whole(query_grad),
        whole(inverse),
        (small, pl.BlockSpec((1, EXTRA, WIDTH), lambda g, pos: (place(g, pos), 4, 0))),
        (text, pl.BlockSpec((1, ROWS, WIDTH), lambda g, pos: (place(g, pos), 0, 0))),
    ]
    shape = jax.ShapeDtypeStruct((SIDE, 2 * WIDTH, COLS), BF)
    outs = [(shape, pl.BlockSpec((1, WIDTH, COLS), lambda g, pos: (g // 2, g % 2, 0)))]
    return call(query_weight_body, pos, (8,), ins, outs, [], 8 * 2**26, 8 * 2**19)[0]


def latent_body(pos, latents, near, far, key_out, value_out):
    for half in range(2):
        left, right = [], []
        for kx in range(SIDE):
            for other in range(2):
                x = lax.rem(pos[0] + kx, SIDE)
                core = 1 - pos[1] if other else pos[1]
                source = (x * CORES + core) * 2 + half
                ky = lax.rem(source // SIDE + SIDE - pos[2], SIDE)
                kz = lax.rem(lax.rem(source, SIDE) + SIDE - pos[3], SIDE)
                left.append(latents[kz * SIDE + ky])
                right.append((far if other else near)[kx])
        total = dot(jnp.concatenate(left, 0), jnp.concatenate(right, 0), (0, 0)).astype(BF)
        rows = slice(half * WIDTH, (half + 1) * WIDTH)
        key_out[rows] = total[:, :COLS]
        value_out[rows] = total[:, COLS:]


def latent_terms(pos, latents, near, far):
    ins = [
        (latents, pl.BlockSpec((16, LAT, WIDTH), lambda i, pos: (0, ROWS // LAT, 0))),
        whole(near),
        whole(far),
    ]
    outs = [whole_out((2 * WIDTH, COLS), BF), whole_out((2 * WIDTH, COLS), BF)]
    return call(latent_body, pos, (1,), ins, outs, [], 2**30, 3 * 2**20)


def shards(
    text_hidden,
    norm_gain,
    gate_alpha,
    latents,
    query_weight,
    key_weight,
    value_weight,
    out_weight,
    citations,
    image_slot,
    out_grad,
):
    place, lane = lax.axis_index("dp"), lax.axis_index("tensor")
    x, core = place // CORES, place % CORES
    y, z = lane // SIDE, lane % SIDE
    pos = jnp.stack([x, core, y, z]).astype(jnp.int32)
    own_latents = latents.reshape(LAT, WIDTH)

    tanh_gate = jnp.tanh(gate_alpha)
    upstream = out_grad.astype(F32)
    own_branch_grad = (upstream * tanh_gate).astype(BF)
    cited = jnp.take(image_slot, citations, axis=0).reshape(-1)
    slots = (cited // CORES + SIDE - x) % SIDE * CORES + (cited + core) % CORES
    slots = slots.astype(jnp.int32)

    slice_latents = send_latents_home(own_latents)
    gain_rows = jnp.broadcast_to(norm_gain[None, :], (EXTRA, WIDTH))
    small = jnp.stack(gather_direct(jnp.concatenate([own_latents, gain_rows], 0), send_z))
    text = jnp.stack(gather_direct(text_hidden, send_z))
    grads = jnp.stack(gather_direct(jnp.concatenate([own_branch_grad, slice_latents], 0), send_y))
    small, text, grads = hold(small, text, grads)

    grads_above, grads_below = send_z(grads, -1), send_z(grads, 1)
    small = jnp.concatenate(gather_direct(small, send_y), 0)
    text_above, text_below = send_y(text, -1), send_y(text, 1)

    total = query_part(pos, [text], [(0, 0)], small, query_weight, (), False)
    grad_total = grad_part(pos, [grads], [(0, 0)], out_weight, (), False)
    pair = own_pair(pos, small, key_weight, value_weight)
    pair = jnp.stack([pair, send_core(pair)])

    grads_above, grads_below, text_above, text_below, pair, total, grad_total = hold(
        grads_above, grads_below, text_above, text_below, pair, total, grad_total
    )
    grads_low, grads_high = send_z(grads_below[:2], 1), send_z(grads_above[2:], -1)
    text_low, text_high = send_y(text_below[:2], 1), send_y(text_above[2:], -1)
    pair = jnp.concatenate(gather_direct(pair, send_x), 0)
    total = query_part(
        pos, [text_above, text_below], [(1, 0), (3, 0)], small, query_weight, total, False
    )
    grad_total = grad_part(
        pos, [grads_above, grads_below], [(1, 0), (3, 0)], out_weight, grad_total, False
    )
    queries, inverse = query_part(
        pos, [text_low, text_high], [(2, 0), (2, 2)], small, query_weight, total, True
    )
    attended_grad = grad_part(
        pos, [grads_low, grads_high], [(2, 0), (2, 2)], out_weight, grad_total, True
    )[0]
    all_text = jnp.concatenate([text, text_above, text_low, text_high, text_below], 0)
    all_grads = jnp.concatenate([grads, grads_above, grads_low, grads_high, grads_below], 0)

    attended, query_grad, pair_kept, pair_given, row_dot = attention(
        slots, queries, attended_grad, pair
    )

    branch_low, branch_high = branch_parts(pos, attended, out_weight, 2, [(2, 0), (2, 2)])
    normed_low, normed_high = normed_parts(
        pos, query_grad, row_dot, query_weight, 2, [(2, 0), (2, 2)]
    )
    branch_low, branch_high = send_y(branch_low, 1), send_y(branch_high, -1)
    normed_low, normed_high = send_z(normed_low, 1), send_z(normed_high, -1)
    branch_up, branch_down = branch_parts(pos, attended, out_weight, 4, [(1, 0), (3, 0)])
    normed_up, normed_down = normed_parts(
        pos, query_grad, row_dot, query_weight, 4, [(1, 0), (3, 0)]
    )
    out_given = out_weight_terms(pos, attended, all_grads, True)
    branch_up = jnp.concatenate([add(branch_up[:2], branch_low).astype(BF), branch_up[2:]], 0)
    branch_down = jnp.concatenate(
        [branch_down[:2], add(branch_down[2:], branch_high).astype(BF)], 0
    )
    normed_up = jnp.concatenate([add(normed_up[:2], normed_low).astype(BF), normed_up[2:]], 0)
    normed_down = jnp.concatenate(
        [normed_down[:2], add(normed_down[2:], normed_high).astype(BF)], 0
    )
    branch_up, branch_down, normed_up, normed_down = hold(
        branch_up, branch_down, normed_up, normed_down
    )
    branch_up, branch_down = send_y(branch_up, 1), send_y(branch_down, -1)
    normed_up, normed_down = send_z(normed_up, 1), send_z(normed_down, -1)
    branch_own = branch_parts(pos, attended, out_weight, 4, [(0, 0)])[0]
    normed_own = normed_parts(pos, query_grad, row_dot, query_weight, 4, [(0, 0)])[0]

    def over_x(kept, arrived):
        block = [add(kept[k], arrived[k]).astype(BF) for k in range(SIDE)]
        arrived = [send_x(block[1], 1), send_x(block[3], -1), send_x(block[2], 2)]
        return add(block[0], *arrived).astype(BF)

    out_kept = out_weight_terms(pos, attended, all_grads, False)
    out_weight_grad = over_x(out_kept, send_core(out_given))
    query_given = query_weight_terms(pos, query_grad, inverse, small, all_text, True)
    query_kept = query_weight_terms(pos, query_grad, inverse, small, all_text, False)
    query_weight_grad = over_x(query_kept, send_core(query_given))

    near = add(pair_kept, send_core(pair_given)).astype(BF)
    arrived = [near]
    for d, by in ((1, -1), (2, 2), (3, 1)):
        arrived.append(jnp.roll(send_x(near, by), d, axis=0))
    near = add(*arrived).astype(BF)
    far = send_core(near)
    key_weight_grad, value_weight_grad = latent_terms(pos, all_grads, near, far)

    def second(own, up, down, send):
        block = [add(own[k], up[k], down[k]) for k in range(SIDE)]
        sent = [value.astype(BF) for value in block]
        return add(block[0], send(sent[2], 2), send(sent[1], 1), send(sent[3], -1))

    branch = second(branch_own, branch_up, branch_down, send_z)
    normed_sum = second(normed_own, normed_up, normed_down, send_y)
    layer_out = (tanh_gate * branch).astype(BF)
    gate_part = jnp.sum(upstream * branch, axis=0) * (1.0 - tanh_gate * tanh_gate)

    normed_grad, row_sum = normed_sum[:ROWS], normed_sum[ROWS, :ROWS]
    inverse = inverse[:, :1]
    own_unit = text_hidden.astype(F32) * inverse
    unit_grad = normed_grad * norm_gain.astype(F32)
    text_grad = ((unit_grad - own_unit * (row_sum / D)[:, None]) * inverse).astype(BF)
    gain_part = jnp.sum(normed_grad * own_unit, axis=0)
    sums = jnp.stack([gain_part, gate_part])
    sums = sums + send_core(sums)
    sums = sums + send_x(sums, 1) + send_x(sums, -1) + send_x(sums, 2)
    return (
        layer_out,
        text_grad,
        query_weight_grad,
        key_weight_grad,
        value_weight_grad,
        out_weight_grad,
        sums[0],
        sums[1],
    )


def solution(mesh):
    placed = (
        P("dp", "tensor"),
        P("tensor"),
        P("tensor"),
        P("dp", None, "tensor"),
        P(None, "tensor"),
        P(None, "tensor"),
        P(None, "tensor"),
        P("tensor", None),
        P("dp", None),
        P(),
        P("dp", "tensor"),
    )
    return jax.shard_map(
        shards,
        mesh=mesh,
        in_specs=placed,
        out_specs=(
            P("dp", "tensor"),
            P("dp", "tensor"),
            P("dp", "tensor"),
            P("dp", "tensor"),
            P("dp", "tensor"),
            P("tensor", "dp"),
            P("tensor"),
            P("tensor"),
        ),
        check_vma=False,
    )
```

```python
import functools

import jax
import jax.numpy as jnp
from jax import lax
from jax.experimental import pallas as pl
from jax.experimental.pallas import tpu as pltpu
from jax.sharding import PartitionSpec as P

D = 8192
HEAD_DIM = 128
SIDE = 4
CORES = 2
LAT = 64
ROWS = 256
WIDTH = 512
COLS = 256
EXTRA = 16
EPSILON = 1e-05
COST = 64
SCALE = HEAD_DIM ** (-0.5)

BF = jnp.bfloat16
F32 = jnp.float32


def dot(left, right, over):
    return lax.dot_general(left, right, ((over[:1], over[1:]), ((), ())), preferred_element_type=F32)


def ring_send(value, by, axis):
    moves = []
    for x in range(SIDE):
        for core in range(CORES):
            for y in range(SIDE):
                for z in range(SIDE):
                    to = {"x": x, "y": y, "z": z}
                    to[axis] = (to[axis] + (by if core == 0 else -by)) % SIDE
                    source = ((x * CORES + core) * SIDE + y) * SIDE + z
                    target = ((to["x"] * CORES + core) * SIDE + to["y"]) * SIDE + to["z"]
                    moves.append((source, target))
    return lax.ppermute(value, ("dp", "tensor"), moves)


send_x = functools.partial(ring_send, axis="x")
send_y = functools.partial(ring_send, axis="y")
send_z = functools.partial(ring_send, axis="z")


def send_core(value):
    return lax.ppermute(value, "dp", [(i, i ^ 1) for i in range(SIDE * CORES)])


def hold(*values):
    return lax.optimization_barrier(values)


def gather_direct(value, send):
    across, above, below = send(value, 2), send(value, -1), send(value, 1)
    return [value, above, across, below]


def gather_ring(value, send):
    below, above = send(value, 1), send(value, -1)
    return [value, above, send(below, 1), below]


def add(*terms):
    total = terms[0].astype(F32)
    for term in terms[1:]:
        total = total + term.astype(F32)
    return total


def ahead(pos, axis, distance):
    return lax.rem(pos[axis] + (1 - 2 * pos[1]) * distance + SIDE, SIDE)


def distance_to(pos, axis, place):
    return lax.rem((1 - 2 * pos[1]) * (place - pos[axis]) + SIDE, SIDE)


def feature_block(pos, ky, kz):
    return ahead(pos, 2, ky) * SIDE + ahead(pos, 3, kz)


def call(body, pos, grid, ins, outs, scratch, flops, moved, aliases=None):
    arrays, in_specs = zip(*ins)
    shapes, out_specs = zip(*outs)
    return pl.pallas_call(
        body,
        grid_spec=pltpu.PrefetchScalarGridSpec(
            num_scalar_prefetch=1,
            grid=grid,
            in_specs=list(in_specs),
            out_specs=list(out_specs),
            scratch_shapes=scratch,
        ),
        out_shape=list(shapes),
        compiler_params=pltpu.CompilerParams(
            dimension_semantics=("arbitrary",) * len(grid), vmem_limit_bytes=24 * 2**20
        ),
        input_output_aliases=aliases or {},
        cost_estimate=pl.CostEstimate(flops=flops // COST, bytes_accessed=moved // COST, transcendentals=0),
    )(pos, *arrays)


def whole(array):
    zeros = (0,) * array.ndim
    return array, pl.BlockSpec(array.shape, lambda *_: zeros)


def whole_out(shape, dtype):
    zeros = (0,) * len(shape)
    return jax.ShapeDtypeStruct(shape, dtype), pl.BlockSpec(shape, lambda *_: zeros)


def query_body(count, first, last, pos, *refs):
    pieces, gains, weights = refs[:count], refs[count : 2 * count], refs[2 * count : 3 * count]
    rest = refs[3 * count :]
    if not first:
        total_in, squares_in, *rest = rest
    out_a, out_b, total, squares = rest
    step = pl.program_id(0)

    @pl.when(step == 0)
    def _():
        if first:
            total[...] = jnp.zeros_like(total)
            squares[...] = jnp.zeros_like(squares)
        else:
            total[...] = total_in[...]
            squares[...] = squares_in[...]

    for piece, gain, weight in zip(pieces, gains, weights):
        text = piece[0].astype(F32)
        square = text * text
        squares[...] += (square[:, :128] + square[:, 128:256]) + (
            square[:, 256:384] + square[:, 384:]
        )
        scaled = (text * gain[0][:1].astype(F32)).astype(BF)
        total[...] += dot(scaled, weight[...], (1, 0))

    @pl.when(step == pl.num_programs(0) - 1)
    def _():
        if last:
            mean = jnp.sum(squares[...], axis=1, keepdims=True) / D
            inverse = lax.rsqrt(mean + EPSILON)
            out_a[...] = (total[...] * inverse).astype(BF)
            out_b[...] = jnp.broadcast_to(inverse, out_b.shape)
        else:
            out_a[...] = total[...]
            out_b[...] = squares[...]


def query_part(pos, arrays, places, gains, weight, carry, last):
    steps = arrays[0].shape[0]
    ins = [(a, pl.BlockSpec((1, ROWS, WIDTH), lambda i, pos: (i, 0, 0))) for a in arrays]
    for array, at, row in gains:
        index = lambda i, pos, at=at, row=row: (at + i, row // EXTRA, 0)
        ins.append((array, pl.BlockSpec((1, EXTRA, WIDTH), index)))
    for ky, kz in places:
        index = lambda i, pos, ky=ky, kz=kz: (feature_block(pos, ky, kz + i), 0)
        ins.append((weight, pl.BlockSpec((WIDTH, COLS), index)))
    ins += [whole(value) for value in carry]
    outs = [
        whole_out((ROWS, COLS), BF if last else F32),
        whole_out((ROWS, 128), F32),
    ]
    scratch = [pltpu.VMEM((ROWS, COLS), F32), pltpu.VMEM((ROWS, 128), F32)]
    body = functools.partial(query_body, len(arrays), not carry, last)
    work = steps * len(arrays)
    return call(body, pos, (steps,), ins, outs, scratch, work * 2 * ROWS * WIDTH * COLS, work * 2**19)


def grad_body(count, first, last, pos, *refs):
    pieces, weights, rest = refs[:count], refs[count : 2 * count], refs[2 * count :]
    if not first:
        total_in, *rest = rest
    out, total = rest
    step = pl.program_id(0)

    @pl.when(step == 0)
    def _():
        total[...] = jnp.zeros_like(total) if first else total_in[...]

    for piece, weight in zip(pieces, weights):
        total[...] += dot(piece[0], weight[...], (1, 1))

    @pl.when(step == pl.num_programs(0) - 1)
    def _():
        out[...] = total[...].astype(out.dtype)


def grad_part(pos, arrays, places, weight, carry, last):
    steps = arrays[0].shape[0]
    ins = [(a, pl.BlockSpec((1, ROWS, WIDTH), lambda i, pos: (i, 0, 0))) for a in arrays]
    for kz, ky in places:
        index = lambda i, pos, ky=ky, kz=kz: (0, feature_block(pos, ky + i, kz))
        ins.append((weight, pl.BlockSpec((COLS, WIDTH), index)))
    ins += [whole(value) for value in carry]
    outs = [whole_out((ROWS, COLS), BF if last else F32)]
    body = functools.partial(grad_body, len(arrays), not carry, last)
    work = steps * len(arrays)
    scratch = [pltpu.VMEM((ROWS, COLS), F32)]
    return call(body, pos, (steps,), ins, outs, scratch, work * 2 * ROWS * WIDTH * COLS, work * 2**19)


def pair_body(pos, *refs):
    latents, keys, values = refs[:SIDE], refs[SIDE : 2 * SIDE], refs[2 * SIDE : 3 * SIDE]
    out, total = refs[-2:]
    step = pl.program_id(0)

    @pl.when(step == 0)
    def _():
        total[...] = jnp.zeros_like(total)

    def body(rows):
        for kz in range(SIDE):
            total[:, :COLS] += dot(rows[kz], keys[kz][...], (1, 0))
            total[:, COLS:] += dot(rows[kz], values[kz][...], (1, 0))

    at_piece(latents, [1] * SIDE, step, body)

    @pl.when(step == SIDE - 1)
    def _():
        out[...] = total[...].astype(BF)


def at_piece(refs, counts, step, body):
    first = 0
    for ref, count in zip(refs, counts):
        pl.when((step >= first) & (step < first + count))(functools.partial(body, ref))
        first += count


def own_pair(pos, arrays, firsts, key_weight, value_weight):
    ins = []
    for array, first in zip(arrays, firsts):
        index = lambda i, pos, first=first: (0, first // LAT, 0)
        ins.append((array, pl.BlockSpec((SIDE, LAT, WIDTH), index)))
    for weight in (key_weight, value_weight):
        for kz in range(SIDE):
            index = lambda i, pos, kz=kz: (feature_block(pos, i, kz), 0)
            ins.append((weight, pl.BlockSpec((WIDTH, COLS), index)))
    outs = [whole_out((LAT, 2 * COLS), BF)]
    scratch = [pltpu.VMEM((LAT, 2 * COLS), F32)]
    return call(pair_body, pos, (SIDE,), ins, outs, scratch, 2 * LAT * D * 512, 10 * 2**20)[0]


def attention_body(
    pos, queries, grads, pair, inverse, attended, query_grad, scaled, kept, given, row_dot, part
):
    part[...] = jnp.zeros_like(part)
    span = ROWS // 2
    ones = jnp.ones((8, COLS), F32)
    for c in range(2):
        rows = slice(c * span, (c + 1) * span)
        places = [pos[4 + c * 4 + j] for j in range(4)]
        blocks = [pair[at] for at in places]
        product, key_grads, value_grads = [], [], []
        for h in range(2):
            cols = slice(h * HEAD_DIM, (h + 1) * HEAD_DIM)
            value_cols = slice(COLS + h * HEAD_DIM, COLS + (h + 1) * HEAD_DIM)
            keys = jnp.concatenate([block[:, cols] for block in blocks], 0)
            values = jnp.concatenate([block[:, value_cols] for block in blocks], 0)
            query, grad = queries[rows, cols], grads[rows, cols]
            scores = dot(query, keys, (1, 1)) * SCALE
            scores = jnp.exp(scores - jnp.max(scores, axis=1, keepdims=True))
            probs = scores / jnp.sum(scores, axis=1, keepdims=True)
            probs_low = probs.astype(BF)
            attended[rows, cols] = dot(probs_low, values, (1, 0)).astype(BF)
            probs_grad = dot(grad, values, (1, 1))
            inner = jnp.sum(probs * probs_grad, axis=1, keepdims=True)
            score_low = (probs * (probs_grad - inner) * SCALE).astype(BF)
            out = dot(score_low, keys, (1, 0)).astype(BF)
            query_grad[rows, cols] = out
            scaled[rows, cols] = (out.astype(F32) * inverse[rows]).astype(BF)
            product.append(out.astype(F32) * query.astype(F32))
            key_grads.append(dot(score_low, query, (0, 0)))
            value_grads.append(dot(probs_low, grad, (0, 0)))
        pair_grad = jnp.concatenate(key_grads + value_grads, 1)
        for j in range(4):
            part[places[j]] += pair_grad[j * LAT : (j + 1) * LAT]
        line = lax.dot_general(
            ones,
            jnp.concatenate(product, 1),
            (((1,), (1,)), ((), ())),
            precision=lax.Precision.HIGHEST,
            preferred_element_type=F32,
        )
        row_dot[:, rows] = jnp.concatenate([line, line], 0).astype(BF)
    row_dot[:, ROWS:] = jnp.zeros((EXTRA, WIDTH - ROWS), BF)
    for kx in range(SIDE):
        kept[kx] = part[ahead(pos, 0, kx) * CORES + pos[1]].astype(BF)
        given[kx] = part[ahead(pos, 0, (SIDE - kx) % SIDE) * CORES + 1 - pos[1]].astype(BF)


def attention(pos_slots, queries, grads, pair, inverse):
    ins = [whole(queries), whole(grads), whole(pair), whole(inverse)]
    outs = [
        whole_out((ROWS, COLS), BF),
        whole_out((ROWS, COLS), BF),
        whole_out((ROWS, COLS), BF),
        whole_out((SIDE, LAT, 2 * COLS), BF),
        whole_out((SIDE, LAT, 2 * COLS), BF),
        whole_out((EXTRA, WIDTH), BF),
    ]
    scratch = [pltpu.VMEM((SIDE * CORES, LAT, 2 * COLS), F32)]
    return call(attention_body, pos_slots, (1,), ins, outs, scratch, 4 * 10 * 2**23, 3 * 2**20)


def parts_body(count, over, pos, left, *refs):
    weights, rest = refs[:count], refs[count:]
    tail = None
    if len(rest) > count:
        tail, *rest = rest
    for weight, out in zip(weights, rest):
        out[0, :ROWS] = dot(left[...], weight[...], over).astype(BF)
        if tail is not None:
            out[0, ROWS:] = tail[...]


def branch_parts(pos, left, weight, steps, places):
    ins = [whole(left)]
    outs = []
    for ky, kz in places:
        index = lambda i, pos, ky=ky, kz=kz: (0, feature_block(pos, ky, kz + i))
        ins.append((weight, pl.BlockSpec((COLS, WIDTH), index)))
        shape = jax.ShapeDtypeStruct((steps, ROWS, WIDTH), BF)
        outs.append((shape, pl.BlockSpec((1, ROWS, WIDTH), lambda i, pos: (i, 0, 0))))
    body = functools.partial(parts_body, len(places), (1, 0))
    work = steps * len(places)
    return call(body, pos, (steps,), ins, outs, [], work * 2 * ROWS * WIDTH * COLS, work * 2**19)


def normed_parts(pos, left, tail, weight, steps, places):
    ins = [whole(left)]
    outs = []
    for kz, ky in places:
        index = lambda i, pos, ky=ky, kz=kz: (feature_block(pos, ky + i, kz), 0)
        ins.append((weight, pl.BlockSpec((WIDTH, COLS), index)))
        shape = jax.ShapeDtypeStruct((steps, ROWS + EXTRA, WIDTH), BF)
        outs.append((shape, pl.BlockSpec((1, ROWS + EXTRA, WIDTH), lambda i, pos: (i, 0, 0))))
    ins.append(whole(tail))
    body = functools.partial(parts_body, len(places), (1, 1))
    work = steps * len(places)
    return call(body, pos, (steps,), ins, outs, [], work * 2 * ROWS * WIDTH * COLS, work * 2**19)


def half_at(place):
    return pl.ds(pl.multiple_of(lax.rem(place, CORES) * WIDTH, WIDTH), WIDTH)


def spread(arrays):
    spec = pl.BlockSpec((1, ROWS, WIDTH), lambda s, pos: (s, 0, 0))
    return [(array, spec) for array in arrays]


def out_weight_body(pos, attended, *refs):
    for kz in range(SIDE):
        place = ahead(pos, 3, kz)
        value = dot(attended[...], refs[kz][0], (0, 0)).astype(BF)
        refs[-1][0, place // CORES, :, half_at(place)] = value


def out_weight_terms(pos, attended, grads):
    shape = jax.ShapeDtypeStruct((SIDE, CORES, COLS, 2 * WIDTH), BF)
    index = lambda s, pos: (ahead(pos, 2, s), 0, 0, 0)
    outs = [(shape, pl.BlockSpec((1, CORES, COLS, 2 * WIDTH), index))]
    ins = [whole(attended)] + spread(grads)
    out = call(out_weight_body, pos, (SIDE,), ins, outs, [], 16 * 2**26, 16 * 2**19)[0]
    return out.reshape(8, COLS, 2 * WIDTH)


def query_weight_body(pos, query_grad, *refs):
    for ky in range(SIDE):
        refs[-1][ahead(pos, 2, ky), 0] = dot(refs[ky][0], query_grad[...], (0, 0)).astype(BF)


def query_weight_terms(pos, query_grad, text):
    def index(s, pos):
        at = ahead(pos, 3, s)
        return 0, at // CORES, lax.rem(at, CORES), 0

    shape = jax.ShapeDtypeStruct((SIDE, CORES, 2 * WIDTH, COLS), BF)
    outs = [(shape, pl.BlockSpec((SIDE, 1, WIDTH, COLS), index))]
    ins = [whole(query_grad)] + spread(text)
    out = call(query_weight_body, pos, (SIDE,), ins, outs, [], 16 * 2**26, 16 * 2**19)[0]
    return out.reshape(8, 2 * WIDTH, COLS)


def add_body(count, pos, *refs):
    sums, terms, outs = refs[:count], refs[count : 2 * count], refs[2 * count :]
    for total, term, out in zip(sums, terms, outs):
        out[...] = (total[...].astype(F32) + term[...].astype(F32)).astype(BF)


def add_arrived(pos, sums, terms):
    ins, outs = [], []
    for total in sums:
        spec = pl.BlockSpec((1,) + total.shape[1:], lambda i, pos: (i, 0, 0))
        ins.append((total, spec))
        outs.append((jax.ShapeDtypeStruct(total.shape, BF), spec))
    for term in terms:
        ins.append((term, pl.BlockSpec((1,) + term.shape[1:], lambda i, pos: (i, 0, 0))))
    body = functools.partial(add_body, len(sums))
    aliases = {1 + i: i for i in range(len(sums))}
    return call(body, pos, (SIDE,), ins, outs, [], 2**20, 6 * 2**20, aliases)


def slice_body(pos, *refs):
    given, kept = refs[-2:]
    for ky in range(SIDE):
        kx = distance_to(pos, 0, ahead(pos, 2, ky))
        for kz in range(SIDE):
            place = ahead(pos, 3, kz)
            cols = half_at(place)
            mine = place // CORES == pos[1]

            @pl.when(mine)
            def _(ky=ky, kz=kz, kx=kx, cols=cols):
                kept[kx, :, cols] = refs[ky][kz]

            @pl.when(jnp.logical_not(mine))
            def _(ky=ky, kz=kz, kx=kx, cols=cols):
                given[lax.rem(SIDE - kx, SIDE), :, cols] = refs[ky][kz]


def latent_slices(pos, small):
    ins = [(a, pl.BlockSpec((SIDE, LAT, WIDTH), lambda i, pos: (0, 0, 0))) for a in small]
    outs = [whole_out((SIDE, LAT, 2 * WIDTH), BF), whole_out((SIDE, LAT, 2 * WIDTH), BF)]
    return call(slice_body, pos, (1,), ins, outs, [], 2**10, 2**21)


def latent_body(pos, *refs):
    slices, (near, far, key_out, value_out) = refs[:SIDE], refs[SIDE:]
    left, right = [], []
    for kx in range(SIDE):
        left += [slices[kx][0], slices[kx][1]]
        right += [near[kx], far[(SIDE - kx) % SIDE]]
    right = jnp.concatenate(right, 0)
    for half in range(2):
        rows = slice(half * WIDTH, (half + 1) * WIDTH)
        block = jnp.concatenate([part[:, rows] for part in left], 0)
        total = dot(block, right, (0, 0)).astype(BF)
        key_out[rows] = total[:, :COLS]
        value_out[rows] = total[:, COLS:]


def latent_terms(pos, slices, near, far):
    ins = [whole(array) for array in slices] + [whole(near), whole(far)]
    outs = [whole_out((2 * WIDTH, COLS), BF), whole_out((2 * WIDTH, COLS), BF)]
    return call(latent_body, pos, (1,), ins, outs, [], 2**30, 3 * 2**20)


def shards(
    text_hidden,
    norm_gain,
    gate_alpha,
    latents,
    query_weight,
    key_weight,
    value_weight,
    out_weight,
    citations,
    image_slot,
    out_grad,
):
    place, lane = lax.axis_index("dp"), lax.axis_index("tensor")
    x, core = place // CORES, place % CORES
    y, z = lane // SIDE, lane % SIDE
    pos = jnp.stack([x, core, y, z]).astype(jnp.int32)
    own_latents = latents.reshape(LAT, WIDTH)

    tanh_gate = jnp.tanh(gate_alpha)
    upstream = out_grad.astype(F32)
    own_branch_grad = (upstream * tanh_gate).astype(BF)
    cited = jnp.take(image_slot, citations, axis=0).reshape(-1)
    slots = cited.astype(jnp.int32)
    pos_slots = jnp.concatenate([pos, slots])

    gain_rows = jnp.broadcast_to(norm_gain[None, :], (EXTRA, WIDTH))
    packed = gather_ring(jnp.concatenate([text_hidden, own_latents, gain_rows], 0), send_z)
    text = jnp.stack([block[:ROWS] for block in packed])
    small = jnp.stack([block[ROWS:] for block in packed])
    grads = jnp.stack(gather_ring(own_branch_grad, send_y))
    text, small, pos, pos_slots = hold(text, small, pos, pos_slots)

    grads_above, grads_below = send_z(grads, -1), send_z(grads, 1)
    small = gather_direct(small, send_y)
    total = query_part(pos, [text], [(0, 0)], [(small[0], 0, LAT)], query_weight, (), False)
    text, total_a, total_b, *small = hold(text, *total, *small)
    total = (total_a, total_b)
    text_above, text_below = send_y(text, -1), send_y(text, 1)
    pair = own_pair(pos, small, [0] * SIDE, key_weight, value_weight)
    pair = lax.all_gather(pair, "dp", axis=0)
    slices_given, slices_kept = latent_slices(pos, small)
    slices_arrived = send_core(slices_given)
    grad_total = grad_part(pos, [grads], [(0, 0)], out_weight, (), False)
    text_above, text_below, grads_above, grads_below, pair, slices_arrived, *grad_total = hold(
        text_above, text_below, grads_above, grads_below, pair, slices_arrived, *grad_total
    )

    text_across, grads_across = send_y(text_below, 1), send_z(grads_below, 1)
    slices = jnp.stack([slices_kept, slices_arrived], 1)
    slices_3, slices_1 = send_x(slices[1], 1), send_x(slices[3], -1)
    slices = [slices[0], slices_1, send_x(slices[2], 2), slices_3]
    total = query_part(
        pos,
        [text_above, text_below],
        [(1, 0), (3, 0)],
        [(small[1], 0, LAT), (small[3], 0, LAT)],
        query_weight,
        total,
        False,
    )
    grad_total = grad_part(
        pos, [grads_above, grads_below], [(1, 0), (3, 0)], out_weight, grad_total, False
    )
    text_across, grads_across, total_a, total_b, *rest = hold(
        text_across, grads_across, *total, *grad_total, *slices
    )
    grad_total, slices = rest[:1], rest[1:]
    queries, inverse = query_part(
        pos,
        [text_across],
        [(2, 0)],
        [(small[2], 0, LAT)],
        query_weight,
        (total_a, total_b),
        True,
    )
    attended_grad = grad_part(pos, [grads_across], [(2, 0)], out_weight, grad_total, True)[0]
    all_text = [text, text_above, text_across, text_below]
    all_grads = [grads, grads_above, grads_across, grads_below]
    gains = jnp.concatenate([block[:, LAT] for block in small], 0)
    own_gain = []
    for half in range(2):
        t = place * 2 + half
        at = distance_to(pos, 2, t // SIDE) * SIDE + distance_to(pos, 3, t % SIDE)
        own_gain.append(lax.dynamic_index_in_dim(gains, at, 0, keepdims=False))
    own_gain = jnp.concatenate(own_gain).astype(F32)[:, None]

    attended, query_grad, scaled_grad, pair_kept, pair_given, row_dot = attention(
        pos_slots, queries, attended_grad, pair, inverse
    )

    def over_dp(term):
        return lax.psum_scatter(term, "dp", scatter_dimension=0, tiled=True)[0]

    out_weight_grad = over_dp(out_weight_terms(pos, attended, all_grads))
    query_weight_grad = over_dp(query_weight_terms(pos, scaled_grad, all_text))
    query_weight_grad = (query_weight_grad.astype(F32) * own_gain).astype(BF)

    near = add(pair_kept, send_core(pair_given)).astype(BF)
    (branch_2,) = branch_parts(pos, attended, out_weight, SIDE, [(2, 0)])
    (normed_2,) = normed_parts(pos, query_grad, row_dot, query_weight, SIDE, [(2, 0)])
    branch_2, normed_2, attended, query_grad, near = hold(
        branch_2, normed_2, attended, query_grad, near
    )
    branch_2, normed_2 = send_y(branch_2, 1), send_z(normed_2, 1)
    near_3, near_1, near_2 = send_x(near, 1), send_x(near, -1), send_x(near, 2)
    branch_1, branch_3 = branch_parts(pos, attended, out_weight, SIDE, [(1, 0), (3, 0)])
    normed_1, normed_3 = normed_parts(
        pos, query_grad, row_dot, query_weight, SIDE, [(1, 0), (3, 0)]
    )
    branch_1, normed_1 = add_arrived(pos, [branch_1, normed_1], [branch_2, normed_2])
    branch_1, branch_3, normed_1, normed_3, attended, query_grad, near_1, near_2, near_3 = hold(
        branch_1, branch_3, normed_1, normed_3, attended, query_grad, near_1, near_2, near_3
    )
    branch_1, normed_1 = send_y(branch_1, 1), send_z(normed_1, 1)
    branch_3, normed_3 = send_y(branch_3, -1), send_z(normed_3, -1)
    (branch_0,) = branch_parts(pos, attended, out_weight, SIDE, [(0, 0)])
    (normed_0,) = normed_parts(pos, query_grad, row_dot, query_weight, SIDE, [(0, 0)])
    near = add(
        near, jnp.roll(near_1, 1, axis=0), jnp.roll(near_2, 2, axis=0), jnp.roll(near_3, 3, axis=0)
    ).astype(BF)
    far = send_core(near)
    branch_0, branch_1, branch_3, normed_0, normed_1, normed_3, near, far = hold(
        branch_0, branch_1, branch_3, normed_0, normed_1, normed_3, near, far
    )

    def second(own, up, down, send):
        block = [add(own[k], up[k], down[k]) for k in range(SIDE)]
        sent = [value.astype(BF) for value in block]
        return add(block[0], send(sent[2], 2), send(sent[1], 1), send(sent[3], -1))

    branch = second(branch_0, branch_1, branch_3, send_z)
    normed_sum = second(normed_0, normed_1, normed_3, send_y)
    layer_out = (tanh_gate * branch).astype(BF)
    gate_part = jnp.sum(upstream * branch, axis=0) * (1.0 - tanh_gate * tanh_gate)

    key_weight_grad, value_weight_grad = latent_terms(pos, slices, near, far)

    normed_grad, row_sum = normed_sum[:ROWS], normed_sum[ROWS, :ROWS]
    inverse = inverse[:, :1]
    own_unit = text_hidden.astype(F32) * inverse
    unit_grad = normed_grad * norm_gain.astype(F32)
    text_grad = ((unit_grad - own_unit * (row_sum / D)[:, None]) * inverse).astype(BF)
    gain_part = jnp.sum(normed_grad * own_unit, axis=0)
    sums = jnp.stack([gain_part, gate_part])
    sums = sums + send_core(sums)
    sums = sums + send_x(sums, 1) + send_x(sums, -1) + send_x(sums, 2)
    return (
        layer_out,
        text_grad,
        query_weight_grad,
        key_weight_grad,
        value_weight_grad,
        out_weight_grad,
        sums[0],
        sums[1],
    )


def solution(mesh):
    placed = (
        P("dp", "tensor"),
        P("tensor"),
        P("tensor"),
        P("dp", None, "tensor"),
        P(None, "tensor"),
        P(None, "tensor"),
        P(None, "tensor"),
        P("tensor", None),
        P("dp", None),
        P(),
        P("dp", "tensor"),
    )
    return jax.shard_map(
        shards,
        mesh=mesh,
        in_specs=placed,
        out_specs=(
            P("dp", "tensor"),
            P("dp", "tensor"),
            P("dp", "tensor"),
            P("dp", "tensor"),
            P("dp", "tensor"),
            P("tensor", "dp"),
            P("tensor"),
            P("tensor"),
        ),
        check_vma=False,
    )
```

```python
import functools

import jax
import jax.numpy as jnp
from jax import lax
from jax.experimental import pallas as pl
from jax.experimental.pallas import tpu as pltpu
from jax.sharding import PartitionSpec as P

D = 8192
HEAD_DIM = 128
SIDE = 4
CORES = 2
LAT = 64
ROWS = 256
WIDTH = 512
COLS = 256
EXTRA = 16
EPSILON = 1e-05
COST = 64
SCALE = HEAD_DIM ** (-0.5)

BF = jnp.bfloat16
F32 = jnp.float32


def dot(left, right, over):
    return lax.dot_general(left, right, ((over[:1], over[1:]), ((), ())), preferred_element_type=F32)


def ring_send(value, by, axis):
    moves = []
    for x in range(SIDE):
        for core in range(CORES):
            for y in range(SIDE):
                for z in range(SIDE):
                    to = {"x": x, "y": y, "z": z}
                    to[axis] = (to[axis] + (by if core == 0 else -by)) % SIDE
                    source = ((x * CORES + core) * SIDE + y) * SIDE + z
                    target = ((to["x"] * CORES + core) * SIDE + to["y"]) * SIDE + to["z"]
                    moves.append((source, target))
    return lax.ppermute(value, ("dp", "tensor"), moves)


send_x = functools.partial(ring_send, axis="x")
send_y = functools.partial(ring_send, axis="y")
send_z = functools.partial(ring_send, axis="z")


def send_core(value):
    return lax.ppermute(value, "dp", [(i, i ^ 1) for i in range(SIDE * CORES)])


def hold(*values):
    return lax.optimization_barrier(values)


def gather_direct(value, send):
    across, above, below = send(value, 2), send(value, -1), send(value, 1)
    return [value, above, across, below]


def gather_ring(value, send):
    below, above = send(value, 1), send(value, -1)
    return [value, above, send(below, 1), below]


def add(*terms):
    total = terms[0].astype(F32)
    for term in terms[1:]:
        total = total + term.astype(F32)
    return total


def ahead(pos, axis, distance):
    return lax.rem(pos[axis] + (1 - 2 * pos[1]) * distance + SIDE, SIDE)


def distance_to(pos, axis, place):
    return lax.rem((1 - 2 * pos[1]) * (place - pos[axis]) + SIDE, SIDE)


def feature_block(pos, ky, kz):
    return ahead(pos, 2, ky) * SIDE + ahead(pos, 3, kz)


def call(body, pos, grid, ins, outs, scratch, flops, moved, aliases=None):
    arrays, in_specs = zip(*ins)
    shapes, out_specs = zip(*outs)
    return pl.pallas_call(
        body,
        grid_spec=pltpu.PrefetchScalarGridSpec(
            num_scalar_prefetch=1,
            grid=grid,
            in_specs=list(in_specs),
            out_specs=list(out_specs),
            scratch_shapes=scratch,
        ),
        out_shape=list(shapes),
        compiler_params=pltpu.CompilerParams(
            dimension_semantics=("arbitrary",) * len(grid), vmem_limit_bytes=12 * 2**20
        ),
        input_output_aliases=aliases or {},
        cost_estimate=pl.CostEstimate(flops=flops // COST, bytes_accessed=moved // COST, transcendentals=0),
    )(pos, *arrays)


def whole(array):
    zeros = (0,) * array.ndim
    return array, pl.BlockSpec(array.shape, lambda *_: zeros)


def whole_out(shape, dtype):
    zeros = (0,) * len(shape)
    return jax.ShapeDtypeStruct(shape, dtype), pl.BlockSpec(shape, lambda *_: zeros)


def query_body(count, first, last, pos, *refs):
    pieces, gains, weights = refs[:count], refs[count : 2 * count], refs[2 * count : 3 * count]
    rest = refs[3 * count :]
    if not first:
        total_in, squares_in, *rest = rest
    out_a, out_b, total, squares = rest
    step = pl.program_id(0)

    @pl.when(step == 0)
    def _():
        if first:
            total[...] = jnp.zeros_like(total)
            squares[...] = jnp.zeros_like(squares)
        else:
            total[...] = total_in[...]
            squares[...] = squares_in[...]

    for piece, gain, weight in zip(pieces, gains, weights):
        text = piece[0].astype(F32)
        square = text * text
        squares[...] += (square[:, :128] + square[:, 128:256]) + (
            square[:, 256:384] + square[:, 384:]
        )
        scaled = (text * gain[0][:1].astype(F32)).astype(BF)
        total[...] += dot(scaled, weight[...], (1, 0))

    @pl.when(step == pl.num_programs(0) - 1)
    def _():
        if last:
            mean = jnp.sum(squares[...], axis=1, keepdims=True) / D
            inverse = lax.rsqrt(mean + EPSILON)
            out_a[...] = (total[...] * inverse).astype(BF)
            out_b[...] = jnp.broadcast_to(inverse, out_b.shape)
        else:
            out_a[...] = total[...]
            out_b[...] = squares[...]


def query_part(pos, arrays, places, gains, weight, carry, last):
    steps = arrays[0].shape[0]
    ins = [(a, pl.BlockSpec((1, ROWS, WIDTH), lambda i, pos: (i, 0, 0))) for a in arrays]
    for array, at, row in gains:
        index = lambda i, pos, at=at, row=row: (at + i, row // EXTRA, 0)
        ins.append((array, pl.BlockSpec((1, EXTRA, WIDTH), index)))
    for ky, kz in places:
        index = lambda i, pos, ky=ky, kz=kz: (feature_block(pos, ky, kz + i), 0)
        ins.append((weight, pl.BlockSpec((WIDTH, COLS), index)))
    ins += [whole(value) for value in carry]
    outs = [
        whole_out((ROWS, COLS), BF if last else F32),
        whole_out((ROWS, 128), F32),
    ]
    scratch = [pltpu.VMEM((ROWS, COLS), F32), pltpu.VMEM((ROWS, 128), F32)]
    body = functools.partial(query_body, len(arrays), not carry, last)
    work = steps * len(arrays)
    return call(body, pos, (steps,), ins, outs, scratch, work * 2 * ROWS * WIDTH * COLS, work * 2**19)


def grad_body(count, first, last, pos, *refs):
    pieces, weights, rest = refs[:count], refs[count : 2 * count], refs[2 * count :]
    if not first:
        total_in, *rest = rest
    out, total = rest
    step = pl.program_id(0)

    @pl.when(step == 0)
    def _():
        total[...] = jnp.zeros_like(total) if first else total_in[...]

    for piece, weight in zip(pieces, weights):
        total[...] += dot(piece[0], weight[...], (1, 1))

    @pl.when(step == pl.num_programs(0) - 1)
    def _():
        out[...] = total[...].astype(out.dtype)


def grad_part(pos, arrays, places, weight, carry, last):
    steps = arrays[0].shape[0]
    ins = [(a, pl.BlockSpec((1, ROWS, WIDTH), lambda i, pos: (i, 0, 0))) for a in arrays]
    for kz, ky in places:
        index = lambda i, pos, ky=ky, kz=kz: (0, feature_block(pos, ky + i, kz))
        ins.append((weight, pl.BlockSpec((COLS, WIDTH), index)))
    ins += [whole(value) for value in carry]
    outs = [whole_out((ROWS, COLS), BF if last else F32)]
    body = functools.partial(grad_body, len(arrays), not carry, last)
    work = steps * len(arrays)
    scratch = [pltpu.VMEM((ROWS, COLS), F32)]
    return call(body, pos, (steps,), ins, outs, scratch, work * 2 * ROWS * WIDTH * COLS, work * 2**19)


def pair_body(pos, *refs):
    latents, keys, values = refs[:SIDE], refs[SIDE : 2 * SIDE], refs[2 * SIDE : 3 * SIDE]
    out, total = refs[-2:]
    step = pl.program_id(0)

    @pl.when(step == 0)
    def _():
        total[...] = jnp.zeros_like(total)

    def body(rows):
        for kz in range(SIDE):
            total[:, :COLS] += dot(rows[kz], keys[kz][...], (1, 0))
            total[:, COLS:] += dot(rows[kz], values[kz][...], (1, 0))

    at_piece(latents, [1] * SIDE, step, body)

    @pl.when(step == SIDE - 1)
    def _():
        out[...] = total[...].astype(BF)


def at_piece(refs, counts, step, body):
    first = 0
    for ref, count in zip(refs, counts):
        pl.when((step >= first) & (step < first + count))(functools.partial(body, ref))
        first += count


def own_pair(pos, arrays, firsts, key_weight, value_weight):
    ins = []
    for array, first in zip(arrays, firsts):
        index = lambda i, pos, first=first: (0, first // LAT, 0)
        ins.append((array, pl.BlockSpec((SIDE, LAT, WIDTH), index)))
    for weight in (key_weight, value_weight):
        for kz in range(SIDE):
            index = lambda i, pos, kz=kz: (feature_block(pos, i, kz), 0)
            ins.append((weight, pl.BlockSpec((WIDTH, COLS), index)))
    outs = [whole_out((LAT, 2 * COLS), BF)]
    scratch = [pltpu.VMEM((LAT, 2 * COLS), F32)]
    return call(pair_body, pos, (SIDE,), ins, outs, scratch, 2 * LAT * D * 512, 10 * 2**20)[0]


def attention_body(
    pos, queries, grads, pair, inverse, attended, query_grad, scaled, kept, given, row_dot, part
):
    part[...] = jnp.zeros_like(part)
    span = ROWS // 2
    ones = jnp.ones((8, COLS), F32)
    for c in range(2):
        rows = slice(c * span, (c + 1) * span)
        places = [pos[4 + c * 4 + j] for j in range(4)]
        blocks = [pair[at] for at in places]
        product, key_grads, value_grads = [], [], []
        for h in range(2):
            cols = slice(h * HEAD_DIM, (h + 1) * HEAD_DIM)
            value_cols = slice(COLS + h * HEAD_DIM, COLS + (h + 1) * HEAD_DIM)
            keys = jnp.concatenate([block[:, cols] for block in blocks], 0)
            values = jnp.concatenate([block[:, value_cols] for block in blocks], 0)
            query, grad = queries[rows, cols], grads[rows, cols]
            scores = dot(query, keys, (1, 1)) * SCALE
            scores = jnp.exp(scores - jnp.max(scores, axis=1, keepdims=True))
            probs = scores / jnp.sum(scores, axis=1, keepdims=True)
            probs_low = probs.astype(BF)
            attended[rows, cols] = dot(probs_low, values, (1, 0)).astype(BF)
            probs_grad = dot(grad, values, (1, 1))
            inner = jnp.sum(probs * probs_grad, axis=1, keepdims=True)
            score_low = (probs * (probs_grad - inner) * SCALE).astype(BF)
            out = dot(score_low, keys, (1, 0)).astype(BF)
            query_grad[rows, cols] = out
            scaled[rows, cols] = (out.astype(F32) * inverse[rows]).astype(BF)
            product.append(out.astype(F32) * query.astype(F32))
            key_grads.append(dot(score_low, query, (0, 0)))
            value_grads.append(dot(probs_low, grad, (0, 0)))
        pair_grad = jnp.concatenate(key_grads + value_grads, 1)
        for j in range(4):
            part[places[j]] += pair_grad[j * LAT : (j + 1) * LAT]
        line = lax.dot_general(
            ones,
            jnp.concatenate(product, 1),
            (((1,), (1,)), ((), ())),
            precision=lax.Precision.HIGHEST,
            preferred_element_type=F32,
        )
        row_dot[:, rows] = jnp.concatenate([line, line], 0).astype(BF)
    row_dot[:, ROWS:] = jnp.zeros((EXTRA, WIDTH - ROWS), BF)
    for kx in range(SIDE):
        kept[kx] = part[ahead(pos, 0, kx) * CORES + pos[1]].astype(BF)
        given[kx] = part[ahead(pos, 0, (SIDE - kx) % SIDE) * CORES + 1 - pos[1]].astype(BF)


def attention(pos_slots, queries, grads, pair, inverse):
    ins = [whole(queries), whole(grads), whole(pair), whole(inverse)]
    outs = [
        whole_out((ROWS, COLS), BF),
        whole_out((ROWS, COLS), BF),
        whole_out((ROWS, COLS), BF),
        whole_out((SIDE, LAT, 2 * COLS), BF),
        whole_out((SIDE, LAT, 2 * COLS), BF),
        whole_out((EXTRA, WIDTH), BF),
    ]
    scratch = [pltpu.VMEM((SIDE * CORES, LAT, 2 * COLS), F32)]
    return call(attention_body, pos_slots, (1,), ins, outs, scratch, 4 * 10 * 2**23, 3 * 2**20)


def parts_body(count, over, pos, left, *refs):
    weights, rest = refs[:count], refs[count:]
    tail = None
    if len(rest) > count:
        tail, *rest = rest
    for weight, out in zip(weights, rest):
        out[0, :ROWS] = dot(left[...], weight[...], over).astype(BF)
        if tail is not None:
            out[0, ROWS:] = tail[...]


def branch_parts(pos, left, weight, steps, places):
    ins = [whole(left)]
    outs = []
    for ky, kz in places:
        index = lambda i, pos, ky=ky, kz=kz: (0, feature_block(pos, ky, kz + i))
        ins.append((weight, pl.BlockSpec((COLS, WIDTH), index)))
        shape = jax.ShapeDtypeStruct((steps, ROWS, WIDTH), BF)
        outs.append((shape, pl.BlockSpec((1, ROWS, WIDTH), lambda i, pos: (i, 0, 0))))
    body = functools.partial(parts_body, len(places), (1, 0))
    work = steps * len(places)
    return call(body, pos, (steps,), ins, outs, [], work * 2 * ROWS * WIDTH * COLS, work * 2**19)


def normed_parts(pos, left, tail, weight, steps, places):
    ins = [whole(left)]
    outs = []
    for kz, ky in places:
        index = lambda i, pos, ky=ky, kz=kz: (feature_block(pos, ky + i, kz), 0)
        ins.append((weight, pl.BlockSpec((WIDTH, COLS), index)))
        shape = jax.ShapeDtypeStruct((steps, ROWS + EXTRA, WIDTH), BF)
        outs.append((shape, pl.BlockSpec((1, ROWS + EXTRA, WIDTH), lambda i, pos: (i, 0, 0))))
    ins.append(whole(tail))
    body = functools.partial(parts_body, len(places), (1, 1))
    work = steps * len(places)
    return call(body, pos, (steps,), ins, outs, [], work * 2 * ROWS * WIDTH * COLS, work * 2**19)


def half_at(place):
    return pl.ds(pl.multiple_of(lax.rem(place, CORES) * WIDTH, WIDTH), WIDTH)


def spread(arrays):
    spec = pl.BlockSpec((1, ROWS, WIDTH), lambda s, pos: (s, 0, 0))
    return [(array, spec) for array in arrays]


def out_weight_body(pos, attended, *refs):
    for kz in range(SIDE):
        place = ahead(pos, 3, kz)
        value = dot(attended[...], refs[kz][0], (0, 0)).astype(BF)
        refs[-1][0, place // CORES, :, half_at(place)] = value


def out_weight_terms(pos, attended, grads):
    shape = jax.ShapeDtypeStruct((SIDE, CORES, COLS, 2 * WIDTH), BF)
    index = lambda s, pos: (ahead(pos, 2, s), 0, 0, 0)
    outs = [(shape, pl.BlockSpec((1, CORES, COLS, 2 * WIDTH), index))]
    ins = [whole(attended)] + spread(grads)
    out = call(out_weight_body, pos, (SIDE,), ins, outs, [], 16 * 2**26, 16 * 2**19)[0]
    return out.reshape(8, COLS, 2 * WIDTH)


def query_weight_body(pos, query_grad, *refs):
    for ky in range(SIDE):
        refs[-1][ahead(pos, 2, ky), 0] = dot(refs[ky][0], query_grad[...], (0, 0)).astype(BF)


def query_weight_terms(pos, query_grad, text):
    def index(s, pos):
        at = ahead(pos, 3, s)
        return 0, at // CORES, lax.rem(at, CORES), 0

    shape = jax.ShapeDtypeStruct((SIDE, CORES, 2 * WIDTH, COLS), BF)
    outs = [(shape, pl.BlockSpec((SIDE, 1, WIDTH, COLS), index))]
    ins = [whole(query_grad)] + spread(text)
    out = call(query_weight_body, pos, (SIDE,), ins, outs, [], 16 * 2**26, 16 * 2**19)[0]
    return out.reshape(8, 2 * WIDTH, COLS)


def slice_body(pos, *refs):
    given, kept = refs[-2:]
    for ky in range(SIDE):
        kx = distance_to(pos, 0, ahead(pos, 2, ky))
        for kz in range(SIDE):
            place = ahead(pos, 3, kz)
            cols = half_at(place)
            mine = place // CORES == pos[1]

            @pl.when(mine)
            def _(ky=ky, kz=kz, kx=kx, cols=cols):
                kept[kx, :, cols] = refs[ky][kz]

            @pl.when(jnp.logical_not(mine))
            def _(ky=ky, kz=kz, kx=kx, cols=cols):
                given[lax.rem(SIDE - kx, SIDE), :, cols] = refs[ky][kz]


def latent_slices(pos, small):
    ins = [(a, pl.BlockSpec((SIDE, LAT, WIDTH), lambda i, pos: (0, 0, 0))) for a in small]
    outs = [whole_out((SIDE, LAT, 2 * WIDTH), BF), whole_out((SIDE, LAT, 2 * WIDTH), BF)]
    return call(slice_body, pos, (1,), ins, outs, [], 2**10, 2**21)


def latent_body(pos, *refs):
    slices, (near, far, key_out, value_out) = refs[:SIDE], refs[SIDE:]
    left, right = [], []
    for kx in range(SIDE):
        left += [slices[kx][0], slices[kx][1]]
        right += [near[kx], far[(SIDE - kx) % SIDE]]
    right = jnp.concatenate(right, 0)
    for half in range(2):
        rows = slice(half * WIDTH, (half + 1) * WIDTH)
        block = jnp.concatenate([part[:, rows] for part in left], 0)
        total = dot(block, right, (0, 0)).astype(BF)
        key_out[rows] = total[:, :COLS]
        value_out[rows] = total[:, COLS:]


def latent_terms(pos, slices, near, far):
    ins = [whole(array) for array in slices] + [whole(near), whole(far)]
    outs = [whole_out((2 * WIDTH, COLS), BF), whole_out((2 * WIDTH, COLS), BF)]
    return call(latent_body, pos, (1,), ins, outs, [], 2**30, 3 * 2**20)


def shards(
    text_hidden,
    norm_gain,
    gate_alpha,
    latents,
    query_weight,
    key_weight,
    value_weight,
    out_weight,
    citations,
    image_slot,
    out_grad,
):
    place, lane = lax.axis_index("dp"), lax.axis_index("tensor")
    x, core = place // CORES, place % CORES
    y, z = lane // SIDE, lane % SIDE
    pos = jnp.stack([x, core, y, z]).astype(jnp.int32)
    own_latents = latents.reshape(LAT, WIDTH)

    tanh_gate = jnp.tanh(gate_alpha)
    upstream = out_grad.astype(F32)
    own_branch_grad = (upstream * tanh_gate).astype(BF)
    cited = jnp.take(image_slot, citations, axis=0).reshape(-1)
    slots = cited.astype(jnp.int32)
    pos_slots = jnp.concatenate([pos, slots])

    gain_rows = jnp.broadcast_to(norm_gain[None, :], (EXTRA, WIDTH))
    packed = gather_ring(jnp.concatenate([text_hidden, own_latents, gain_rows], 0), send_z)
    text = jnp.stack([block[:ROWS] for block in packed])
    small = jnp.stack([block[ROWS:] for block in packed])
    grads = jnp.stack(gather_ring(own_branch_grad, send_y))
    text, small, pos, pos_slots = hold(text, small, pos, pos_slots)

    grads_above, grads_below = send_z(grads, -1), send_z(grads, 1)
    small = gather_direct(small, send_y)
    total = query_part(pos, [text], [(0, 0)], [(small[0], 0, LAT)], query_weight, (), False)
    text, total_a, total_b, *small = hold(text, *total, *small)
    total = (total_a, total_b)
    text_above, text_below = send_y(text, -1), send_y(text, 1)
    pair = own_pair(pos, small, [0] * SIDE, key_weight, value_weight)
    pair = lax.all_gather(pair, "dp", axis=0)
    slices_given, slices_kept = latent_slices(pos, small)
    slices_arrived = send_core(slices_given)
    grad_total = grad_part(pos, [grads], [(0, 0)], out_weight, (), False)
    text_above, text_below, grads_above, grads_below, pair, slices_arrived, *grad_total = hold(
        text_above, text_below, grads_above, grads_below, pair, slices_arrived, *grad_total
    )

    text_across, grads_across = send_y(text_below, 1), send_z(grads_below, 1)
    slices = jnp.stack([slices_kept, slices_arrived], 1)
    slices_3, slices_1 = send_x(slices[1], 1), send_x(slices[3], -1)
    slices = [slices[0], slices_1, send_x(slices[2], 2), slices_3]
    total = query_part(
        pos,
        [text_above, text_below],
        [(1, 0), (3, 0)],
        [(small[1], 0, LAT), (small[3], 0, LAT)],
        query_weight,
        total,
        False,
    )
    grad_total = grad_part(
        pos, [grads_above, grads_below], [(1, 0), (3, 0)], out_weight, grad_total, False
    )
    text_across, grads_across, total_a, total_b, *rest = hold(
        text_across, grads_across, *total, *grad_total, *slices
    )
    grad_total, slices = rest[:1], rest[1:]
    queries, inverse = query_part(
        pos,
        [text_across],
        [(2, 0)],
        [(small[2], 0, LAT)],
        query_weight,
        (total_a, total_b),
        True,
    )
    attended_grad = grad_part(pos, [grads_across], [(2, 0)], out_weight, grad_total, True)[0]
    all_text = [text, text_above, text_across, text_below]
    all_grads = [grads, grads_above, grads_across, grads_below]
    gains = jnp.concatenate([block[:, LAT] for block in small], 0)
    own_gain = []
    for half in range(2):
        t = place * 2 + half
        at = distance_to(pos, 2, t // SIDE) * SIDE + distance_to(pos, 3, t % SIDE)
        own_gain.append(lax.dynamic_index_in_dim(gains, at, 0, keepdims=False))
    own_gain = jnp.concatenate(own_gain).astype(F32)[:, None]

    attended, query_grad, scaled_grad, pair_kept, pair_given, row_dot = attention(
        pos_slots, queries, attended_grad, pair, inverse
    )

    def over_dp(term):
        return lax.psum_scatter(term, "dp", scatter_dimension=0, tiled=True)[0]

    out_weight_grad = over_dp(out_weight_terms(pos, attended, all_grads))
    query_weight_grad = over_dp(query_weight_terms(pos, scaled_grad, all_text))
    query_weight_grad = (query_weight_grad.astype(F32) * own_gain).astype(BF)

    near = add(pair_kept, send_core(pair_given)).astype(BF)
    (branch_2,) = branch_parts(pos, attended, out_weight, SIDE, [(2, 0)])
    (normed_2,) = normed_parts(pos, query_grad, row_dot, query_weight, SIDE, [(2, 0)])
    branch_2, normed_2, attended, query_grad, near = hold(
        branch_2, normed_2, attended, query_grad, near
    )
    branch_2, normed_2 = send_y(branch_2, 1), send_z(normed_2, 1)
    near_3, near_1 = send_x(near, 1), send_x(near, -1)
    branch_1, branch_3 = branch_parts(pos, attended, out_weight, SIDE, [(1, 0), (3, 0)])
    normed_1, normed_3 = normed_parts(
        pos, query_grad, row_dot, query_weight, SIDE, [(1, 0), (3, 0)]
    )
    branch_1, normed_1 = add(branch_1, branch_2).astype(BF), add(normed_1, normed_2).astype(BF)
    branch_1, branch_3, normed_1, normed_3, attended, query_grad, near, near_1, near_3 = hold(
        branch_1, branch_3, normed_1, normed_3, attended, query_grad, near, near_1, near_3
    )
    near_2 = send_x(near, 2)
    branch_1, normed_1 = send_y(branch_1, 1), send_z(normed_1, 1)
    branch_3, normed_3 = send_y(branch_3, -1), send_z(normed_3, -1)
    (branch_0,) = branch_parts(pos, attended, out_weight, SIDE, [(0, 0)])
    (normed_0,) = normed_parts(pos, query_grad, row_dot, query_weight, SIDE, [(0, 0)])
    near = add(
        near, jnp.roll(near_1, 1, axis=0), jnp.roll(near_2, 2, axis=0), jnp.roll(near_3, 3, axis=0)
    ).astype(BF)
    far = send_core(near)
    branch_0, branch_1, branch_3, normed_0, normed_1, normed_3, near, far = hold(
        branch_0, branch_1, branch_3, normed_0, normed_1, normed_3, near, far
    )

    def second(own, up, down, send):
        block = [add(own[k], up[k], down[k]) for k in range(SIDE)]
        sent = [value.astype(BF) for value in block]
        return add(block[0], send(sent[2], 2), send(sent[1], 1), send(sent[3], -1))

    branch = second(branch_0, branch_1, branch_3, send_z)
    normed_sum = second(normed_0, normed_1, normed_3, send_y)
    layer_out = (tanh_gate * branch).astype(BF)
    gate_part = jnp.sum(upstream * branch, axis=0) * (1.0 - tanh_gate * tanh_gate)

    key_weight_grad, value_weight_grad = latent_terms(pos, slices, near, far)

    normed_grad, row_sum = normed_sum[:ROWS], normed_sum[ROWS, :ROWS]
    inverse = inverse[:, :1]
    own_unit = text_hidden.astype(F32) * inverse
    unit_grad = normed_grad * norm_gain.astype(F32)
    text_grad = ((unit_grad - own_unit * (row_sum / D)[:, None]) * inverse).astype(BF)
    gain_part = jnp.sum(normed_grad * own_unit, axis=0)
    sums = jnp.stack([gain_part, gate_part])
    sums = sums + send_core(sums)
    sums, query_weight_grad = hold(
        sums + send_x(sums, 1) + send_x(sums, -1) + send_x(sums, 2), query_weight_grad
    )
    return (
        layer_out,
        text_grad,
        query_weight_grad,
        key_weight_grad,
        value_weight_grad,
        out_weight_grad,
        sums[0],
        sums[1],
    )


def solution(mesh):
    placed = (
        P("dp", "tensor"),
        P("tensor"),
        P("tensor"),
        P("dp", None, "tensor"),
        P(None, "tensor"),
        P(None, "tensor"),
        P(None, "tensor"),
        P("tensor", None),
        P("dp", None),
        P(),
        P("dp", "tensor"),
    )
    return jax.shard_map(
        shards,
        mesh=mesh,
        in_specs=placed,
        out_specs=(
            P("dp", "tensor"),
            P("dp", "tensor"),
            P("dp", "tensor"),
            P("dp", "tensor"),
            P("dp", "tensor"),
            P("tensor", "dp"),
            P("tensor"),
            P("tensor"),
        ),
        check_vma=False,
    )
```
